32 devices in a mesh: gx: 8 (over z, y), sa: 4 (over x, core).
Axes of the slice: x: 2, y: 2, z: 4, core: 2. Of those that a mesh axis runs over, the one named last changes fastest.
Arguments:
- gas: float32 [4, 16, 32, 1024], P(None, 'gx', None, 'sa'), may hold values from -6 to 6
- melt: float32 [2, 16, 128, 1024], P(None, 'gx', 'sa'), may hold values from -6 to 6
- surface_mask: int32 [16, 1024], P('gx'), may hold values 0 or 1
- melt_level: int32 [16, 1024], P('gx'), may hold values from 32 to 128
Outputs:
- gas_rate: float32 [4, 16, 32, 1024], P(None, 'gx', None, 'sa')
- melt_rate: float32 [2, 16, 128, 1024], P(None, 'gx', 'sa')
The draws below stay inside these ranges and needn't reach their ends.
Inputs may be any that keep to these rules, and one draw needn't show every extreme that they name: `melt_level`: a level equal to 128 means the column is liquid to the bottom.
All inputs are finite; a program needn't handle non-finite values. No bound on the sum of `surface_mask` on one device may be relied on, other than what follows from the above.
Results may differ from the reference program's by a relative error of at most 0.0003.
Values sent between devices are 32-bit elements; how exact they have to be, the bound alone decides.
No kernel may reach another device: no remote copies, remote signals or barrier semaphores. Data moves between devices by JAX's collectives and lax.ppermute only.
A program may use at most 64 MiB of HBM per device.

```python
import jax
import jax.numpy as jnp
from jax import lax

CX = 2
NZW = 32
SPAN = 1024
DEPTH = 128
NX = 16


def touch_ends(values, stream_key, low, largest):
    extent = values.shape
    place = [jax.random.randint(jax.random.fold_in(stream_key, axis), (), 0, extent[axis]) for axis in range(len(extent))]
    values = values.at[tuple(place)].set(low)
    longest = extent.index(max(extent))
    place[longest] = (place[longest] + 1) % extent[longest]
    return values.at[tuple(place)].set(largest)


def shard_levels(key, dims, split, smallest, largest):
    def one(position, blocks):
        heights = jax.random.uniform(jax.random.fold_in(jax.random.fold_in(key, 6), position), (blocks,), jnp.float32, smallest / len(split), largest / len(split))
        return jnp.repeat(jnp.exp(heights), dims[position] // blocks).reshape((-1,) + (1,) * (len(dims) - position - 1))

    factor_of = one(*split[0])
    for cut in split[1:]:
        factor_of = factor_of * one(*cut)
    return factor_of


def noise(own_key, dims, deviation, bound, shards=(), held_as=jnp.bfloat16):
    gain = shard_levels(own_key, dims, shards, -0.22, 0.18) if shards else 1.0
    values = jax.random.normal(own_key, dims, jnp.float32) * deviation * gain
    return jnp.minimum(jnp.maximum(values, -bound), bound).astype(held_as)


def setup_inputs(seed: int = 0) -> dict:
    key_of = jax.random.split(jax.random.key(seed), 5)
    gas = noise(key_of[0], (4, NX, NZW, SPAN), 1.0, 6.0, ((1, 8), (3, 4)), jnp.float32)
    melt = noise(key_of[1], (2, NX, DEPTH, SPAN), 1.0, 6.0, ((1, 8), (2, 4)), jnp.float32)
    surface_mask = touch_ends((jax.random.randint(key_of[2], (NX, SPAN), 0, 4) < 3).astype(jnp.int32), jax.random.fold_in(key_of[2], 1), 0, 1)
    melt_level = touch_ends(jax.random.randint(key_of[3], (NX, SPAN), DEPTH // 4, DEPTH + 1), jax.random.fold_in(key_of[3], 1), DEPTH // 4, DEPTH).astype(jnp.int32)
    return {"gas": gas, "melt": melt, "surface_mask": surface_mask, "melt_level": melt_level}


gas_viscosity = 0.05
gas_diffusivity = 0.07
turbulent_prandtl = 0.85
melt_viscosity = 0.2
melt_diffusivity = 0.5
epsilon = 1e-06

def wall_pad(source):
    return jnp.concatenate([-source[..., 0:1, :], source, source[..., -1:, :]], axis=-2)

def strip_margin(source, width):
    return source[..., width:source.shape[-3] - width, :, width:source.shape[-1] - width]

def gradients(source):
    padded = wall_pad(source)
    along_x = 0.5 * (source[..., 2:, :, 1:-1] - source[..., :-2, :, 1:-1])
    along_y = 0.5 * (source[..., 1:-1, :, 2:] - source[..., 1:-1, :, :-2])
    along_z = 0.5 * (padded[..., 1:-1, 2:, 1:-1] - padded[..., 1:-1, :-2, 1:-1])
    return jnp.stack([along_x, along_y, along_z], axis=-4)

def test_filter(source):
    along = 0.25 * source[..., :-2, :, :] + 0.5 * source[..., 1:-1, :, :] + 0.25 * source[..., 2:, :, :]
    return 0.25 * along[..., :-2] + 0.5 * along[..., 1:-1] + 0.25 * along[..., 2:]

def laplacian(source):
    padded = wall_pad(source)
    middle = source[..., 1:-1, :, 1:-1]
    beside_all = source[..., 2:, :, 1:-1] + source[..., :-2, :, 1:-1] + source[..., 1:-1, :, 2:] + source[..., 1:-1, :, :-2]
    return beside_all + padded[..., 1:-1, 2:, 1:-1] + padded[..., 1:-1, :-2, 1:-1] - 6.0 * middle

def strain_of(gradient):
    strain = 0.5 * (gradient + jnp.swapaxes(gradient, 0, 1))
    magnitude = jnp.sqrt(2.0 * lax.optimization_barrier(jnp.sum(strain * strain, axis=(0, 1))))
    return (strain, magnitude)

def germano_parts(velocity):
    gradient = gradients(velocity)
    strain, magnitude = strain_of(gradient)
    inner = strip_margin(velocity, 1)
    resolved_filtered = test_filter(magnitude * strain)
    pair_filtered = test_filter(inner[:, None] * inner[None, :])
    coarse_velocity = test_filter(velocity)
    coarse_strain, coarse_magnitude = strain_of(gradients(coarse_velocity))
    coarse_inner = strip_margin(coarse_velocity, 1)
    leonard = pair_filtered - coarse_inner[:, None] * coarse_inner[None, :]
    model_term = resolved_filtered - 4.0 * coarse_magnitude * coarse_strain
    numerator = lax.optimization_barrier(jnp.sum(leonard * model_term, axis=(0, 1, 4)))
    denominator = lax.optimization_barrier(jnp.sum(model_term * model_term, axis=(0, 1, 4)))
    return (numerator, denominator, gradient, magnitude)

def lilly_coefficient(numerator, denominator, span_cells):
    mean_numerator = numerator / span_cells
    mean_denominator = denominator / span_cells
    return -mean_numerator / (2.0 * (mean_denominator + epsilon))

def gas_rates(velocity, heat_field, gradient, magnitude, coefficient):
    inner_magnitude = strip_margin(magnitude, 1)
    eddy = coefficient[:, :, None] * inner_magnitude
    inner_velocity = strip_margin(velocity, 2)
    inner_gradient = strip_margin(gradient, 1)
    advection = lax.optimization_barrier(jnp.sum(inner_velocity[None, :] * inner_gradient, axis=1))
    momentum = -advection + (gas_viscosity + eddy) * laplacian(strip_margin(velocity, 1))
    heat_gradient = gradients(heat_field)
    transport = lax.optimization_barrier(jnp.sum(inner_velocity * heat_gradient, axis=0))
    energy = -transport + (gas_diffusivity + eddy / turbulent_prandtl) * laplacian(heat_field)
    section_rate = jnp.concatenate([momentum, energy[None]], axis=0)
    planes = (inner_velocity[0, :, 0, :], strip_margin(heat_field, 1)[:, 0, :], inner_magnitude[:, 0, :])
    return (section_rate, planes)

def wall_fluxes(streamwise_plane, heat_plane, magnitude_plane, wall_coefficient):
    eddy = wall_coefficient[:, None] * magnitude_plane
    wall_shear = (gas_viscosity + eddy) * 2.0 * streamwise_plane
    wall_heat = (gas_diffusivity + eddy / turbulent_prandtl) * 2.0 * heat_plane
    return (wall_shear, wall_heat)

def upper_ghost(top_rows, surface_mask):
    streamwise = jnp.where(surface_mask == 1, top_rows[0], -top_rows[0])
    return jnp.stack([streamwise, top_rows[1]])

def melt_rates(x_upper, x_lower, depth_padded, surface_mask, melt_level, depth_index, wall_shear, wall_heat):
    centre = depth_padded[:, :, 1:-1, :]
    beside_all = x_upper + x_lower + depth_padded[:, :, 2:, :] + depth_padded[:, :, :-2, :]
    beside_all = beside_all + jnp.roll(centre, 1, axis=-1) + jnp.roll(centre, -1, axis=-1)
    laplace = beside_all - 6.0 * centre
    surface = (depth_index == 0).astype(jnp.float32)[None, :, None]
    liquid_share = surface_mask.astype(jnp.float32)
    momentum = melt_viscosity * laplace[0] + surface * (liquid_share * wall_shear)[:, None, :]
    solid = depth_index[None, :, None] >= melt_level[:, None, :]
    momentum = jnp.where(solid, jnp.zeros_like(momentum), momentum)
    energy = melt_diffusivity * laplace[1] + surface * wall_heat[:, None, :]
    return jnp.stack([momentum, energy])

def reference(gas, melt, surface_mask, melt_level):

    def one_block(block_index):
        first_row = block_index * CX
        row_ids = ((first_row - 2 + jnp.arange(CX + 4, dtype=jnp.int32)) % NX).astype(jnp.int32)
        gas_block = jnp.take(gas, row_ids, axis=1)
        gas_block = jnp.concatenate([gas_block[..., -2:], gas_block, gas_block[..., :2]], axis=-1)
        velocity = gas_block[:3]
        heat_field = strip_margin(gas_block[3], 1)
        numerator, denominator, gradient, magnitude = germano_parts(velocity)
        coefficient = lilly_coefficient(numerator, denominator, float(SPAN))
        section_rate, planes = gas_rates(velocity, heat_field, gradient, magnitude, coefficient)
        wall_shear, wall_heat = wall_fluxes(planes[0], planes[1], planes[2], coefficient[:, 0])
        melt_ids = ((first_row - 1 + jnp.arange(CX + 2, dtype=jnp.int32)) % NX).astype(jnp.int32)
        melt_block = jnp.take(melt, melt_ids, axis=1)
        block_mask = lax.dynamic_slice_in_dim(surface_mask, first_row, CX, 0)
        block_level = lax.dynamic_slice_in_dim(melt_level, first_row, CX, 0)
        centre = melt_block[:, 1:-1]
        upper_row = upper_ghost(centre[:, :, 0, :], block_mask)
        depth_padded = jnp.concatenate([upper_row[:, :, None], centre, centre[:, :, -1:, :]], axis=2)
        depth_index = jnp.arange(DEPTH, dtype=jnp.int32)
        melt_section = melt_rates(melt_block[:, 2:], melt_block[:, :-2], depth_padded, block_mask, block_level, depth_index, wall_shear, wall_heat)
        return (section_rate, melt_section)
    gas_blocks, melt_blocks = lax.map(one_block, jnp.arange(NX // CX, dtype=jnp.int32))
    gas_rate = jnp.moveaxis(gas_blocks, 0, 1).reshape(4, NX, NZW, SPAN)
    melt_rate = jnp.moveaxis(melt_blocks, 0, 1).reshape(2, NX, DEPTH, SPAN)
    return (gas_rate, melt_rate)
```

```python
import functools

import jax
import jax.numpy as jnp
from jax import lax
from jax.experimental import pallas as pl
from jax.experimental.pallas import tpu as pltpu
from jax.sharding import PartitionSpec as P

gas_viscosity = 0.05
gas_diffusivity = 0.07
turbulent_prandtl = 0.85
melt_viscosity = 0.2
melt_diffusivity = 0.5
epsilon = 1e-06

LANES = 128
SUB = 8
EDGE = 4
PAIRS = ((0, 0), (1, 1), (2, 2), (0, 1), (0, 2), (1, 2))
VMEM = pl.BlockSpec(memory_space=pltpu.VMEM)


def shift_lanes(source, amount):
    extent = source.shape[-1]
    return pltpu.roll(source, amount % extent, source.ndim - 1)


def slot(row_block, cell, component, cells):
    return ((row_block * cells + cell) * 4 + component) * EDGE


def pack_gas(gas_ref, edge_ref):
    _, cells, rows, span = gas_ref.shape
    lane = lax.broadcasted_iota(jnp.int32, (SUB, LANES), 1)
    tile = jnp.zeros((SUB, LANES), jnp.float32)
    for block in range(rows // SUB):
        for cell in range(cells):
            for component in range(4):
                at = slot(block, cell, component, cells)
                here = pl.ds(SUB * block, SUB)
                first = gas_ref[component, cell, here, 0:LANES]
                last = gas_ref[component, cell, here, span - LANES : span]
                tile = jnp.where((lane >= at) & (lane < at + 2), shift_lanes(first, at), tile)
                tile = jnp.where(
                    (lane >= at + 2) & (lane < at + 4), shift_lanes(last, at + 4), tile
                )
    edge_ref[...] = tile


def pack_melt(melt_ref, first_ref, last_ref, rows_ref):
    components, cells, depth, _ = melt_ref.shape
    first_ref[...] = melt_ref[:, 0]
    last_ref[...] = melt_ref[:, cells - 1]
    for component in range(components):
        for cell in range(cells):
            at = component * cells + cell
            rows_ref[0, at : at + 1, :] = melt_ref[component, cell, 0:1, :]
            rows_ref[1, at : at + 1, :] = melt_ref[component, cell, depth - 1 : depth, :]


def binomial(source):
    pair = source + shift_lanes(source, 1)
    return pair + shift_lanes(pair, -1)


def germano(own_ref, left_ref, right_ref, below_ref, above_ref, base_ref, eddy_ref, sums_ref, field, coarse, strength):
    _, cells, rows, span = own_ref.shape
    wide = span + LANES
    lane = lax.broadcasted_iota(jnp.int32, (SUB, LANES), 1)
    for index in range(cells + 4):
        if index < 2:
            source, group, cell = left_ref, 0, index + cells - 2
        elif index < cells + 2:
            source, group, cell = own_ref, 1, index - 2
        else:
            source, group, cell = right_ref, 2, index - cells - 2
        for component in range(4 if 1 <= index <= cells + 2 else 3):
            for block in range(rows // SUB):
                at = slot(block, cell, component, cells)
                place = pl.ds(SUB * (block + 1), SUB)
                field[index, component, place, 0:span] = source[
                    component, cell, SUB * block : SUB * (block + 1), :
                ]
                field[index, component, place, span:wide] = jnp.where(
                    lane < LANES // 2,
                    shift_lanes(above_ref[group], -at),
                    shift_lanes(below_ref[group], LANES - 4 - at),
                )
            field[index, component, SUB - 1 : SUB, :] = -field[index, component, SUB : SUB + 1, :]
            field[index, component, SUB + rows : SUB + rows + 1, :] = field[
                index, component, SUB + rows - 1 : SUB + rows, :
            ]

    def filter_block(block, carry):
        place = pl.ds(pl.multiple_of(SUB * (block + 1), SUB), SUB)
        for component in range(3):
            pair = [
                field[i, component, place, :] + field[i + 1, component, place, :]
                for i in range(cells + 3)
            ]
            for i in range(cells + 2):
                coarse[i, component, place, :] = binomial(pair[i] + pair[i + 1])
        return carry

    lax.fori_loop(0, rows // SUB, filter_block, 0)
    for i in range(cells + 2):
        for component in range(3):
            coarse[i, component, SUB - 1 : SUB, :] = -coarse[i, component, SUB : SUB + 1, :]
            coarse[i, component, SUB + rows : SUB + rows + 1, :] = coarse[
                i, component, SUB + rows - 1 : SUB + rows, :
            ]

    row = lax.broadcasted_iota(jnp.int32, (SUB, wide), 0)

    def around(ref, index, component, block):
        previous, place, following = (
            pl.ds(pl.multiple_of(SUB * (block + step), SUB), SUB) for step in range(3)
        )
        middle = ref[index, component, place, :]
        below = jnp.where(row == SUB - 1, ref[index, component, previous, :], middle)
        above = jnp.where(row == 0, ref[index, component, following, :], middle)
        return (
            middle,
            (ref[index - 1, component, place, :], ref[index + 1, component, place, :]),
            (shift_lanes(middle, 1), shift_lanes(middle, -1)),
            (pltpu.roll(below, 1, 0), pltpu.roll(above, SUB - 1, 0)),
        )

    def strain(gradient):
        parts = [
            gradient[i][i] if i == j else gradient[i][j] + gradient[j][i] for i, j in PAIRS
        ]
        diagonal = parts[0] * parts[0] + parts[1] * parts[1] + parts[2] * parts[2]
        off = parts[3] * parts[3] + parts[4] * parts[4] + parts[5] * parts[5]
        return parts, jnp.sqrt(0.5 * diagonal + 0.25 * off)

    column = lax.broadcasted_iota(jnp.int32, (SUB, LANES), 1)

    def rate_block(block, carry):
        out_rows = pl.ds(pl.multiple_of(SUB * block, SUB), SUB)
        place = pl.ds(pl.multiple_of(SUB * (block + 1), SUB), SUB)
        stressed = []
        for index in range(1, cells + 3):
            points = [around(field, index, c, block) for c in range(3)]
            gradient = [[p[1 + j][1] - p[1 + j][0] for j in range(3)] for p in points]
            parts, magnitude = strain(gradient)
            stressed.append([magnitude * part for part in parts])
            if 2 <= index < cells + 2:
                cell = index - 2
                points = points + [around(field, index, 3, block)]
                gradient = gradient + [[points[3][1 + j][1] - points[3][1 + j][0] for j in range(3)]]
                speed = [0.5 * points[j][0][:, :span] for j in range(3)]
                own_magnitude = magnitude[:, :span]
                strength[cell, out_rows, :] = own_magnitude
                for c in range(4):
                    middle, along, across, upward = points[c]
                    laplace = (
                        (along[0] + along[1]) + (across[0] + across[1]) + (upward[0] + upward[1])
                    )[:, :span] - 6.0 * middle[:, :span]
                    advection = (
                        speed[0] * gradient[c][0][:, :span]
                        + speed[1] * gradient[c][1][:, :span]
                        + speed[2] * gradient[c][2][:, :span]
                    )
                    molecular = gas_viscosity if c < 3 else gas_diffusivity
                    base_ref[c, cell, out_rows, :] = molecular * laplace - advection
                    eddy = own_magnitude * laplace
                    eddy_ref[c, cell, out_rows, :] = eddy if c < 3 else eddy * (1.0 / turbulent_prandtl)
        filtered = []
        for k, (i, j) in enumerate(PAIRS):
            pair = [stressed[x][k] + stressed[x + 1][k] for x in range(cells + 1)]
            filtered.append([binomial(pair[x] + pair[x + 1])[:, :span] for x in range(cells)])
        products = []
        for i, j in PAIRS:
            values = [
                field[x, i, place, :] * field[x, j, place, :] for x in range(1, cells + 3)
            ]
            pair = [values[x] + values[x + 1] for x in range(cells + 1)]
            products.append([binomial(pair[x] + pair[x + 1])[:, :span] for x in range(cells)])
        tile = jnp.zeros((SUB, LANES), jnp.float32)
        for cell in range(cells):
            points = [around(coarse, cell + 1, c, block) for c in range(3)]
            gradient = [[(p[1 + j][1] - p[1 + j][0])[:, :span] for j in range(3)] for p in points]
            parts, magnitude = strain(gradient)
            quarter = 0.25 * magnitude
            speed = [0.25 * p[0][:, :span] for p in points]
            numerator = diagonal = off = 0.0
            for k, (i, j) in enumerate(PAIRS):
                model = filtered[k][cell] - quarter * parts[k]
                leonard = products[k][cell] - speed[i] * speed[j]
                numerator = numerator + leonard * model
                if i == j:
                    diagonal = diagonal + model * model
                else:
                    off = off + model * model
            denominator = diagonal + 0.5 * off
            total = jnp.sum(numerator, axis=1, keepdims=True) * (1.0 / 512.0)
            tile = jnp.where(column == cell, total, tile)
            total = jnp.sum(denominator, axis=1, keepdims=True) * (1.0 / 1024.0)
            tile = jnp.where(column == cells + cell, total, tile)
        sums_ref[out_rows, :] = tile
        return carry

    lax.fori_loop(0, rows // SUB, rate_block, 0)
    tiles = span // LANES
    for cell in range(cells):
        planes = (
            strength[cell, 0:1, :],
            own_ref[0, cell, 0:1, :],
            own_ref[3, cell, 0:1, :],
        )
        for p, plane in enumerate(planes):
            for t in range(tiles):
                at = rows + (p * cells + cell) * tiles + t
                sums_ref[at : at + 1, :] = plane[:, t * LANES : (t + 1) * LANES]
    used = rows + 3 * cells * tiles
    if used < sums_ref.shape[0]:
        sums_ref[used:, :] = jnp.zeros((sums_ref.shape[0] - used, LANES), jnp.float32)


def lilly(total, cells, span_cells):
    mean_numerator = total / span_cells
    mean_denominator = shift_lanes(total, -cells) / span_cells
    return -mean_numerator / (2.0 * (mean_denominator + epsilon))


def finish_gas(span_cells, devices, base_ref, eddy_ref, *refs):
    messages, out_ref = refs[:devices], refs[devices]
    _, cells, rows, _ = base_ref.shape
    total = messages[0][0:rows, :]
    for message in messages[1:]:
        total = total + message[0:rows, :]
    coefficient = lilly(total, cells, span_cells)
    for cell in range(cells):
        factor = coefficient[:, cell : cell + 1]
        for component in range(4):
            out_ref[component, cell] = base_ref[component, cell] + factor * eddy_ref[component, cell]


def finish_melt(
    span_cells, devices, rows, span, place_ref, melt_ref, left_ref, right_ref, below_ref, above_ref, mask_ref, level_ref, *refs
):
    messages, out_ref = refs[:devices], refs[devices]
    _, cells, depth, width = melt_ref.shape
    position = place_ref[0]
    total = messages[0][0:SUB, :]
    for message in messages[1:]:
        total = total + message[0:SUB, :]
    coefficient = lilly(total, cells, span_cells)
    tiles = span // LANES
    level_id = lax.broadcasted_iota(jnp.int32, (SUB, width), 0)
    for cell in range(cells):
        factor = coefficient[0:1, cell : cell + 1]
        planes = [
            jnp.concatenate(
                [
                    message[at : at + 1, :]
                    for message in messages
                    for at in range(rows + (p * cells + cell) * tiles, rows + (p * cells + cell + 1) * tiles)
                ],
                axis=1,
            )
            for p in range(3)
        ]
        eddy = factor * planes[0]
        mask = mask_ref[cell : cell + 1, :]
        shear = mask.astype(jnp.float32) * ((gas_viscosity + eddy) * 2.0 * planes[1])
        heat = (gas_diffusivity + eddy / turbulent_prandtl) * 2.0 * planes[2]
        top = position == 0
        shear = jnp.where(top, shear, 0.0)
        heat = jnp.where(top, heat, 0.0)
        levels = level_ref[cell : cell + 1, :]
        for component in range(2):
            at = component * cells + cell
            first = melt_ref[component, cell, 0:1, :]
            ghost = jnp.where(mask == 1, first, -first) if component == 0 else first
            upper = jnp.where(top, ghost, below_ref[at : at + 1, :])
            final = melt_ref[component, cell, depth - 1 : depth, :]
            lower = jnp.where(position == place_ref[1] - 1, final, above_ref[at : at + 1, :])
            for block in range(depth // SUB):
                here = slice(SUB * block, SUB * (block + 1))
                middle = melt_ref[component, cell, here, :]
                over = (
                    jnp.where(level_id == 0, upper, pltpu.roll(middle, 1, 0))
                    if block == 0
                    else melt_ref[component, cell, SUB * block - 1 : SUB * (block + 1) - 1, :]
                )
                under = (
                    jnp.where(level_id == SUB - 1, lower, pltpu.roll(middle, SUB - 1, 0))
                    if block == depth // SUB - 1
                    else melt_ref[component, cell, SUB * block + 1 : SUB * (block + 1) + 1, :]
                )
                before = left_ref[component, here, :] if cell == 0 else melt_ref[component, cell - 1, here, :]
                after = (
                    right_ref[component, here, :]
                    if cell == cells - 1
                    else melt_ref[component, cell + 1, here, :]
                )
                laplace = (before + after) + (over + under)
                laplace = laplace + (shift_lanes(middle, 1) + shift_lanes(middle, -1)) - 6.0 * middle
                rate = (melt_viscosity if component == 0 else melt_diffusivity) * laplace
                if block == 0:
                    rate = rate + jnp.where(level_id == 0, shear if component == 0 else heat, 0.0)
                if component == 0:
                    index = position * depth + SUB * block + level_id
                    rate = jnp.where(index >= levels, 0.0, rate)
                out_ref[component, cell, here, :] = rate


def ring(source, axis, step):
    count = lax.axis_size(axis)
    return lax.ppermute(source, axis, [(i, (i + step) % count) for i in range(count)])


def exchange(source, axis):
    count = lax.axis_size(axis)
    if count & (count - 1):
        return [source] + [ring(source, axis, -k) for k in range(1, count)]
    return [source] + [
        lax.ppermute(source, axis, [(i, i ^ k) for i in range(count)]) for k in range(1, count)
    ]


def call(kernel, outs, scratch=(), specs=None):
    return pl.pallas_call(
        kernel,
        out_shape=outs,
        in_specs=specs,
        out_specs=jax.tree.map(lambda _: VMEM, outs),
        scratch_shapes=scratch,
        compiler_params=pltpu.CompilerParams(vmem_limit_bytes=24 * 1024 * 1024),
    )


def array(*shape):
    return jax.ShapeDtypeStruct(shape, jnp.float32)


def on_device(gas, melt, surface_mask, melt_level):
    _, cells, rows, span = gas.shape
    _, _, depth, width = melt.shape
    devices = lax.axis_size("sa")
    span_cells = float(span * devices)
    gas_left = ring(gas, "gx", 1)
    gas_right = ring(gas, "gx", -1)
    edges = call(pack_gas, array(SUB, LANES), specs=[VMEM])(gas)
    edges = jnp.stack([ring(edges, "gx", 1), edges, ring(edges, "gx", -1)])
    below = ring(edges, "sa", 1)
    above = ring(edges, "sa", -1)
    first, last, depth_rows = call(
        pack_melt,
        (array(2, depth, width), array(2, depth, width), array(2, 2 * cells, width)),
        specs=[VMEM],
    )(melt)
    upper = ring(depth_rows[1], "sa", 1)
    lower = ring(depth_rows[0], "sa", -1)
    gas_left, gas_right, first, last = lax.optimization_barrier((gas_left, gas_right, first, last))
    melt_left = ring(last, "gx", 1)
    melt_right = ring(first, "gx", -1)
    wide = span + LANES
    used = rows + 3 * cells * (span // LANES)
    message_rows = -(-used // SUB) * SUB
    base, eddy, message = call(
        germano,
        (array(4, cells, rows, span), array(4, cells, rows, span), array(message_rows, LANES)),
        scratch=(
            pltpu.VMEM((cells + 4, 4, rows + 2 * SUB, wide), jnp.float32),
            pltpu.VMEM((cells + 2, 3, rows + 2 * SUB, wide), jnp.float32),
            pltpu.VMEM((cells, rows, span), jnp.float32),
        ),
        specs=[VMEM] * 5,
    )(gas, gas_left, gas_right, below, above)
    messages = exchange(message, "sa")
    gas_rate = call(
        functools.partial(finish_gas, span_cells, devices),
        array(4, cells, rows, span),
        specs=[VMEM] * (2 + devices),
    )(base, eddy, *messages)
    place = jnp.stack([lax.axis_index("sa"), devices]).astype(jnp.int32)
    melt_rate = call(
        functools.partial(finish_melt, span_cells, devices, rows, span),
        array(2, cells, depth, width),
        specs=[pl.BlockSpec(memory_space=pltpu.SMEM)] + [VMEM] * (7 + devices),
    )(place, melt, melt_left, melt_right, upper, lower, surface_mask, melt_level, *messages)
    return (gas_rate, melt_rate)


def solution(mesh):
    in_specs = (P(None, "gx", None, "sa"), P(None, "gx", "sa", None), P("gx", None), P("gx", None))
    out_specs = (P(None, "gx", None, "sa"), P(None, "gx", "sa", None))
    return jax.shard_map(
        on_device, mesh=mesh, in_specs=in_specs, out_specs=out_specs, check_vma=False
    )
```

```python
import functools

import jax
import jax.numpy as jnp
from jax import lax
from jax.experimental import pallas as pl
from jax.experimental.pallas import tpu as pltpu
from jax.sharding import PartitionSpec as P

gas_viscosity = 0.05
gas_diffusivity = 0.07
turbulent_prandtl = 0.85
melt_viscosity = 0.2
melt_diffusivity = 0.5
epsilon = 1e-06

LANES = 128
SUB = 8
EDGE = 4
PAIRS = ((0, 0), (1, 1), (2, 2), (0, 1), (0, 2), (1, 2))
VMEM = pl.BlockSpec(memory_space=pltpu.VMEM)
SMEM = pl.BlockSpec(memory_space=pltpu.SMEM)
ANY = pl.BlockSpec(memory_space=pl.ANY)


def shift_lanes(source, amount):
    extent = source.shape[-1]
    return pltpu.roll(source, amount % extent, source.ndim - 1)


def slot(row_block, cell, component, cells):
    return ((row_block * cells + cell) * 4 + component) * EDGE


def pack_sides(place_ref, gas_ref, melt_ref, mate_ref, cross_ref):
    _, cells, rows, span = gas_ref.shape
    components, _, depth, width = melt_ref.shape
    lane = lax.broadcasted_iota(jnp.int32, (SUB, LANES), 1)
    tile = jnp.zeros((SUB, LANES), jnp.float32)
    for block in range(rows // SUB):
        for cell in range(cells):
            for component in range(4):
                at = slot(block, cell, component, cells)
                here = pl.ds(SUB * block, SUB)
                first = gas_ref[component, cell, here, 0:LANES]
                last = gas_ref[component, cell, here, span - LANES : span]
                tile = jnp.where((lane >= at) & (lane < at + 2), shift_lanes(first, at), tile)
                tile = jnp.where(
                    (lane >= at + 2) & (lane < at + 4), shift_lanes(last, at + 4), tile
                )
    mate_ref[0:SUB, :] = tile
    cross_ref[0:SUB, :] = tile
    even = place_ref[0] % 2 == 0
    for component in range(components):
        for cell in range(cells):
            first = melt_ref[component, cell, 0:1, :]
            last = melt_ref[component, cell, depth - 1 : depth, :]
            mate = jnp.where(even, last, first)
            cross = jnp.where(even, first, last)
            for t in range(width // LANES):
                at = SUB + t * components * cells + component * cells + cell
                mate_ref[at : at + 1, :] = mate[:, t * LANES : (t + 1) * LANES]
                cross_ref[at : at + 1, :] = cross[:, t * LANES : (t + 1) * LANES]


def pack_melt(place_ref, melt_ref, after_ref, mate_ref, cross_ref):
    last = melt_ref.shape[1] - 1
    even = place_ref[1] % 2 == 0

    @pl.when(even)
    def _():
        mate_ref[...] = melt_ref[:, last]
        cross_ref[...] = melt_ref[:, 0]

    @pl.when(jnp.logical_not(even))
    def _():
        mate_ref[...] = melt_ref[:, 0]
        cross_ref[...] = melt_ref[:, last]


def binomial(source):
    pair = source + shift_lanes(source, 1)
    return pair + shift_lanes(pair, -1)


def germano(
    place_ref,
    own_ref,
    mate_ref,
    cross_ref,
    halo_ref,
    halo_mate_ref,
    halo_cross_ref,
    base_ref,
    eddy_ref,
    sums_ref,
    field,
    coarse,
    strength,
):
    _, cells, rows, span = own_ref.shape
    wide = span + LANES
    lane = lax.broadcasted_iota(jnp.int32, (SUB, LANES), 1)
    even = place_ref[1] % 2 == 0
    halo = halo_ref[...]
    halo_left = jnp.where(even, halo_cross_ref[...], halo_mate_ref[...])
    halo_right = jnp.where(even, halo_mate_ref[...], halo_cross_ref[...])
    for index in range(cells + 4):
        if index < 2:
            columns, cell = halo_left, index + cells - 2
            sources = cross_ref, mate_ref
        elif index < cells + 2:
            columns, cell = halo, index - 2
            sources = own_ref, own_ref
        else:
            columns, cell = halo_right, index - cells - 2
            sources = mate_ref, cross_ref
        for component in range(4 if 1 <= index <= cells + 2 else 3):
            for block in range(rows // SUB):
                at = slot(block, cell, component, cells)
                place = pl.ds(SUB * (block + 1), SUB)
                here = slice(SUB * block, SUB * (block + 1))
                field[index, component, place, 0:span] = jnp.where(
                    even, sources[0][component, cell, here, :], sources[1][component, cell, here, :]
                )
                field[index, component, place, span:wide] = jnp.where(
                    lane < LANES // 2,
                    shift_lanes(columns, -at),
                    shift_lanes(columns, LANES - 4 - at),
                )
            field[index, component, SUB - 1 : SUB, :] = -field[index, component, SUB : SUB + 1, :]
            field[index, component, SUB + rows : SUB + rows + 1, :] = field[
                index, component, SUB + rows - 1 : SUB + rows, :
            ]

    def filter_block(block, carry):
        place = pl.ds(pl.multiple_of(SUB * (block + 1), SUB), SUB)
        for component in range(3):
            pair = [
                field[i, component, place, :] + field[i + 1, component, place, :]
                for i in range(cells + 3)
            ]
            for i in range(cells + 2):
                coarse[i, component, place, :] = binomial(pair[i] + pair[i + 1])
        return carry

    lax.fori_loop(0, rows // SUB, filter_block, 0)
    for i in range(cells + 2):
        for component in range(3):
            coarse[i, component, SUB - 1 : SUB, :] = -coarse[i, component, SUB : SUB + 1, :]
            coarse[i, component, SUB + rows : SUB + rows + 1, :] = coarse[
                i, component, SUB + rows - 1 : SUB + rows, :
            ]

    row = lax.broadcasted_iota(jnp.int32, (SUB, wide), 0)

    def around(ref, index, component, block):
        previous, place, following = (
            pl.ds(pl.multiple_of(SUB * (block + step), SUB), SUB) for step in range(3)
        )
        middle = ref[index, component, place, :]
        below = jnp.where(row == SUB - 1, ref[index, component, previous, :], middle)
        above = jnp.where(row == 0, ref[index, component, following, :], middle)
        return (
            middle,
            (ref[index - 1, component, place, :], ref[index + 1, component, place, :]),
            (shift_lanes(middle, 1), shift_lanes(middle, -1)),
            (pltpu.roll(below, 1, 0), pltpu.roll(above, SUB - 1, 0)),
        )

    def strain(gradient):
        parts = [
            gradient[i][i] if i == j else gradient[i][j] + gradient[j][i] for i, j in PAIRS
        ]
        diagonal = parts[0] * parts[0] + parts[1] * parts[1] + parts[2] * parts[2]
        off = parts[3] * parts[3] + parts[4] * parts[4] + parts[5] * parts[5]
        return parts, jnp.sqrt(0.5 * diagonal + 0.25 * off)

    column = lax.broadcasted_iota(jnp.int32, (SUB, LANES), 1)

    def rate_block(block, carry):
        out_rows = pl.ds(pl.multiple_of(SUB * block, SUB), SUB)
        place = pl.ds(pl.multiple_of(SUB * (block + 1), SUB), SUB)
        stressed = []
        for index in range(1, cells + 3):
            points = [around(field, index, c, block) for c in range(3)]
            gradient = [[p[1 + j][1] - p[1 + j][0] for j in range(3)] for p in points]
            parts, magnitude = strain(gradient)
            stressed.append([magnitude * part for part in parts])
            if 2 <= index < cells + 2:
                cell = index - 2
                points = points + [around(field, index, 3, block)]
                gradient = gradient + [[points[3][1 + j][1] - points[3][1 + j][0] for j in range(3)]]
                speed = [0.5 * points[j][0][:, :span] for j in range(3)]
                own_magnitude = magnitude[:, :span]
                strength[cell, out_rows, :] = own_magnitude
                for c in range(4):
                    middle, along, across, upward = points[c]
                    laplace = (
                        (along[0] + along[1]) + (across[0] + across[1]) + (upward[0] + upward[1])
                    )[:, :span] - 6.0 * middle[:, :span]
                    advection = (
                        speed[0] * gradient[c][0][:, :span]
                        + speed[1] * gradient[c][1][:, :span]
                        + speed[2] * gradient[c][2][:, :span]
                    )
                    molecular = gas_viscosity if c < 3 else gas_diffusivity
                    base_ref[c, cell, out_rows, :] = molecular * laplace - advection
                    eddy = own_magnitude * laplace
                    eddy_ref[c, cell, out_rows, :] = eddy if c < 3 else eddy * (1.0 / turbulent_prandtl)
        filtered = []
        for k, (i, j) in enumerate(PAIRS):
            pair = [stressed[x][k] + stressed[x + 1][k] for x in range(cells + 1)]
            filtered.append([binomial(pair[x] + pair[x + 1])[:, :span] for x in range(cells)])
        products = []
        for i, j in PAIRS:
            values = [
                field[x, i, place, :] * field[x, j, place, :] for x in range(1, cells + 3)
            ]
            pair = [values[x] + values[x + 1] for x in range(cells + 1)]
            products.append([binomial(pair[x] + pair[x + 1])[:, :span] for x in range(cells)])
        tile = jnp.zeros((SUB, LANES), jnp.float32)
        for cell in range(cells):
            points = [around(coarse, cell + 1, c, block) for c in range(3)]
            gradient = [[(p[1 + j][1] - p[1 + j][0])[:, :span] for j in range(3)] for p in points]
            parts, magnitude = strain(gradient)
            quarter = 0.25 * magnitude
            speed = [0.25 * p[0][:, :span] for p in points]
            numerator = diagonal = off = 0.0
            for k, (i, j) in enumerate(PAIRS):
                model = filtered[k][cell] - quarter * parts[k]
                leonard = products[k][cell] - speed[i] * speed[j]
                numerator = numerator + leonard * model
                if i == j:
                    diagonal = diagonal + model * model
                else:
                    off = off + model * model
            denominator = diagonal + 0.5 * off
            total = jnp.sum(numerator, axis=1, keepdims=True) * (1.0 / 512.0)
            tile = jnp.where(column == cell, total, tile)
            total = jnp.sum(denominator, axis=1, keepdims=True) * (1.0 / 1024.0)
            tile = jnp.where(column == cells + cell, total, tile)
        sums_ref[out_rows, :] = tile
        return carry

    lax.fori_loop(0, rows // SUB, rate_block, 0)
    tiles = span // LANES
    for cell in range(cells):
        planes = (
            strength[cell, 0:1, :],
            own_ref[0, cell, 0:1, :],
            own_ref[3, cell, 0:1, :],
        )
        for p, plane in enumerate(planes):
            for t in range(tiles):
                at = rows + (p * cells + cell) * tiles + t
                sums_ref[at : at + 1, :] = plane[:, t * LANES : (t + 1) * LANES]
    used = rows + 3 * cells * tiles
    if used < sums_ref.shape[0]:
        sums_ref[used:, :] = jnp.zeros((sums_ref.shape[0] - used, LANES), jnp.float32)


def lilly(total, cells, span_cells):
    mean_numerator = total / span_cells
    mean_denominator = shift_lanes(total, -cells) / span_cells
    return -mean_numerator / (2.0 * (mean_denominator + epsilon))


def finish_gas(span_cells, mine_ref, theirs_ref, base_ref, eddy_ref, out_ref):
    _, cells, rows, _ = base_ref.shape
    coefficient = lilly(mine_ref[0:rows, :] + theirs_ref[0:rows, :], cells, span_cells)
    for cell in range(cells):
        factor = coefficient[:, cell : cell + 1]
        for component in range(4):
            out_ref[component, cell] = base_ref[component, cell] + factor * eddy_ref[component, cell]


def finish_melt(
    span_cells,
    devices,
    rows,
    span,
    place_ref,
    mine_ref,
    theirs_ref,
    melt_ref,
    beside_mate_ref,
    beside_cross_ref,
    mate_ref,
    cross_ref,
    mask_ref,
    level_ref,
    out_ref,
):
    components, cells, depth, width = melt_ref.shape
    position = place_ref[0]
    even = position % 2 == 0
    even_cell = place_ref[1] % 2 == 0
    coefficient = lilly(mine_ref[0:SUB, :] + theirs_ref[0:SUB, :], cells, span_cells)
    tiles = span // LANES
    held = (mine_ref.shape[0] - rows) // (devices // 2)
    level_id = lax.broadcasted_iota(jnp.int32, (SUB, width), 0)

    def row_of(ref, at):
        step = components * cells
        return jnp.concatenate(
            [ref[at + t * step : at + t * step + 1, :] for t in range(width // LANES)], axis=1
        )

    for cell in range(cells):
        factor = coefficient[0:1, cell : cell + 1]
        planes = []
        for p in range(3):
            parts = []
            for device in range(devices):
                ref = mine_ref if device < devices // 2 else theirs_ref
                at = rows + device % (devices // 2) * held + (p * cells + cell) * tiles
                parts = parts + [ref[at + t : at + t + 1, :] for t in range(tiles)]
            planes.append(jnp.concatenate(parts, axis=1))
        eddy = factor * planes[0]
        mask = mask_ref[cell : cell + 1, :]
        shear = mask.astype(jnp.float32) * ((gas_viscosity + eddy) * 2.0 * planes[1])
        heat = (gas_diffusivity + eddy / turbulent_prandtl) * 2.0 * planes[2]
        top = position == 0
        shear = jnp.where(top, shear, 0.0)
        heat = jnp.where(top, heat, 0.0)
        levels = level_ref[cell : cell + 1, :]
        for component in range(components):
            at = SUB + component * cells + cell
            from_mate, from_cross = row_of(mate_ref, at), row_of(cross_ref, at)
            first = melt_ref[component, cell, 0:1, :]
            ghost = jnp.where(mask == 1, first, -first) if component == 0 else first
            upper = jnp.where(top, ghost, jnp.where(even, from_cross, from_mate))
            final = melt_ref[component, cell, depth - 1 : depth, :]
            lower = jnp.where(position == devices - 1, final, jnp.where(even, from_mate, from_cross))
            for block in range(depth // SUB):
                here = slice(SUB * block, SUB * (block + 1))
                middle = melt_ref[component, cell, here, :]
                over = (
                    jnp.where(level_id == 0, upper, pltpu.roll(middle, 1, 0))
                    if block == 0
                    else melt_ref[component, cell, SUB * block - 1 : SUB * (block + 1) - 1, :]
                )
                under = (
                    jnp.where(level_id == SUB - 1, lower, pltpu.roll(middle, SUB - 1, 0))
                    if block == depth // SUB - 1
                    else melt_ref[component, cell, SUB * block + 1 : SUB * (block + 1) + 1, :]
                )
                before = (
                    jnp.where(
                        even_cell,
                        beside_cross_ref[component, here, :],
                        beside_mate_ref[component, here, :],
                    )
                    if cell == 0
                    else melt_ref[component, cell - 1, here, :]
                )
                after = (
                    jnp.where(
                        even_cell,
                        beside_mate_ref[component, here, :],
                        beside_cross_ref[component, here, :],
                    )
                    if cell == cells - 1
                    else melt_ref[component, cell + 1, here, :]
                )
                laplace = (before + after) + (over + under)
                laplace = laplace + (shift_lanes(middle, 1) + shift_lanes(middle, -1)) - 6.0 * middle
                rate = (melt_viscosity if component == 0 else melt_diffusivity) * laplace
                if block == 0:
                    rate = rate + jnp.where(level_id == 0, shear if component == 0 else heat, 0.0)
                if component == 0:
                    index = position * depth + SUB * block + level_id
                    rate = jnp.where(index >= levels, 0.0, rate)
                out_ref[component, cell, here, :] = rate


def swap(source, axis, mask):
    return lax.ppermute(source, axis, [(i, i ^ mask) for i in range(lax.axis_size(axis))])


def swap_across(source, axis):
    count = lax.axis_size(axis)
    pairs = [(i, (i + 1) % count) for i in range(1, count, 2)]
    return lax.ppermute(source, axis, pairs + [(j, i) for i, j in pairs])


def exchange(message, rows, axis):
    count = lax.axis_size(axis)
    mask = 1
    while True:
        other = swap(message, axis, mask)
        mask = 2 * mask
        if mask == count:
            return message, other
        message = jnp.concatenate([message[:rows] + other[:rows], message[rows:], other[rows:]])


def fenced(place, part, *arrays):
    def no_part(*arrays):
        shapes = jax.eval_shape(part, *arrays)
        return jax.tree.map(lambda leaf: jnp.zeros(leaf.shape, leaf.dtype), shapes)

    return lax.cond(place[0] < lax.axis_size("sa"), part, no_part, *arrays)


def call(kernel, outs, specs, scratch=(), flops=1):
    return pl.pallas_call(
        kernel,
        out_shape=outs,
        in_specs=specs,
        out_specs=jax.tree.map(lambda _: VMEM, outs),
        scratch_shapes=scratch,
        compiler_params=pltpu.CompilerParams(vmem_limit_bytes=24 * 1024 * 1024),
        cost_estimate=pl.CostEstimate(flops=flops, bytes_accessed=1, transcendentals=0),
    )


def array(*shape):
    return jax.ShapeDtypeStruct(shape, jnp.float32)


def on_device(gas, melt, surface_mask, melt_level):
    _, cells, rows, span = gas.shape
    components, _, depth, width = melt.shape
    devices = lax.axis_size("sa")
    assert devices & (devices - 1) == 0 and devices > 1
    span_cells = float(span * devices)
    place = jnp.stack([lax.axis_index("sa"), lax.axis_index("gx")]).astype(jnp.int32)
    even = place[0] % 2 == 0
    gas_mate, gas_cross = swap(gas, "gx", 1), swap_across(gas, "gx")
    side = array(SUB + components * cells * width // LANES, LANES)
    mate, cross = call(pack_sides, (side, side), [SMEM, VMEM, VMEM])(place, gas, melt)
    mate, cross = swap(mate, "sa", 1), swap_across(cross, "sa")
    late = lax.broadcasted_iota(jnp.int32, (SUB, LANES), 1) % EDGE >= EDGE // 2
    halo = jnp.where(late == even, cross[:SUB], mate[:SUB])
    halo_mate, halo_cross = swap(halo, "gx", 1), swap_across(halo, "gx")
    part = array(components, depth, width)
    beside_mate, beside_cross = call(pack_melt, (part, part), [SMEM, VMEM, ANY])(place, melt, halo)
    beside_mate, beside_cross = swap(beside_mate, "gx", 1), swap_across(beside_cross, "gx")

    def gas_part(*arrays):
        wide = span + LANES
        used = rows + 3 * cells * (span // LANES)
        message_rows = -(-used // SUB) * SUB
        base, eddy, message = call(
            germano,
            (array(4, cells, rows, span), array(4, cells, rows, span), array(message_rows, LANES)),
            [SMEM] + [VMEM] * 6,
            scratch=(
                pltpu.VMEM((cells + 4, 4, rows + 2 * SUB, wide), jnp.float32),
                pltpu.VMEM((cells + 2, 3, rows + 2 * SUB, wide), jnp.float32),
                pltpu.VMEM((cells, rows, span), jnp.float32),
            ),
        )(*arrays)
        return base, eddy, *exchange(message, rows, "sa")

    base, eddy, mine, theirs = fenced(
        place, gas_part, place, gas, gas_mate, gas_cross, halo, halo_mate, halo_cross
    )
    gas_rate = call(
        functools.partial(finish_gas, span_cells), array(4, cells, rows, span), [VMEM] * 4, flops=4000000000
    )(mine, theirs, base, eddy)
    melt_rate = call(
        functools.partial(finish_melt, span_cells, devices, rows, span),
        array(components, cells, depth, width),
        [SMEM] + [VMEM] * 9,
    )(
        place,
        mine,
        theirs,
        melt,
        beside_mate,
        beside_cross,
        mate,
        cross,
        surface_mask,
        melt_level,
    )
    return (gas_rate, melt_rate)


def solution(mesh):
    in_specs = (P(None, "gx", None, "sa"), P(None, "gx", "sa", None), P("gx", None), P("gx", None))
    out_specs = (P(None, "gx", None, "sa"), P(None, "gx", "sa", None))
    return jax.shard_map(
        on_device, mesh=mesh, in_specs=in_specs, out_specs=out_specs, check_vma=False
    )
```

```python
import functools

import jax
import jax.numpy as jnp
from jax import lax
from jax.experimental import pallas as pl
from jax.experimental.pallas import tpu as pltpu
from jax.sharding import PartitionSpec as P

gas_viscosity = 0.05
gas_diffusivity = 0.07
turbulent_prandtl = 0.85
melt_viscosity = 0.2
melt_diffusivity = 0.5
epsilon = 1e-06

LANES = 128
SUB = 8
EDGE = 4
PAIRS = ((0, 0), (1, 1), (2, 2), (0, 1), (0, 2), (1, 2))
VMEM = pl.BlockSpec(memory_space=pltpu.VMEM)
SMEM = pl.BlockSpec(memory_space=pltpu.SMEM)
ANY = pl.BlockSpec(memory_space=pl.ANY)
HBM = pl.BlockSpec(memory_space=pltpu.HBM)


def shift_lanes(source, amount):
    extent = source.shape[-1]
    return pltpu.roll(source, amount % extent, source.ndim - 1)


def slot(row_block, cell, component, cells):
    return ((row_block * cells + cell) * 4 + component) * EDGE


def pack_sides(place_ref, gas_hbm, melt_hbm, mate_ref, cross_ref, gas_ref, ends_ref, sems):
    _, cells, rows, span = gas_ref.shape
    components, _, depth, width = melt_hbm.shape
    copies = [pltpu.make_async_copy(gas_hbm, gas_ref, sems.at[0])]
    for end, start in enumerate((0, depth - SUB)):
        levels = melt_hbm.at[:, :, pl.ds(start, SUB), :]
        copies.append(pltpu.make_async_copy(levels, ends_ref.at[end], sems.at[end + 1]))
    for copy in copies:
        copy.start()
    copies[0].wait()
    lane = lax.broadcasted_iota(jnp.int32, (SUB, LANES), 1)
    tile = jnp.zeros((SUB, LANES), jnp.float32)
    for block in range(rows // SUB):
        for cell in range(cells):
            for component in range(4):
                at = slot(block, cell, component, cells)
                here = pl.ds(SUB * block, SUB)
                first = gas_ref[component, cell, here, 0:LANES]
                last = gas_ref[component, cell, here, span - LANES : span]
                tile = jnp.where((lane >= at) & (lane < at + 2), shift_lanes(first, at), tile)
                tile = jnp.where(
                    (lane >= at + 2) & (lane < at + 4), shift_lanes(last, at + 4), tile
                )
    mate_ref[0:SUB, :] = tile
    cross_ref[0:SUB, :] = tile
    even = place_ref[0] % 2 == 0
    for copy in copies[1:]:
        copy.wait()
    for component in range(components):
        for cell in range(cells):
            first = ends_ref[0, component, cell, 0:1, :]
            last = ends_ref[1, component, cell, SUB - 1 : SUB, :]
            mate = jnp.where(even, last, first)
            cross = jnp.where(even, first, last)
            for t in range(width // LANES):
                at = SUB + t * components * cells + component * cells + cell
                mate_ref[at : at + 1, :] = mate[:, t * LANES : (t + 1) * LANES]
                cross_ref[at : at + 1, :] = cross[:, t * LANES : (t + 1) * LANES]


def pack_melt(place_ref, melt_ref, after_ref, mate_ref, cross_ref):
    last = melt_ref.shape[1] - 1
    even = place_ref[1] % 2 == 0

    @pl.when(even)
    def _():
        mate_ref[...] = melt_ref[:, last]
        cross_ref[...] = melt_ref[:, 0]

    @pl.when(jnp.logical_not(even))
    def _():
        mate_ref[...] = melt_ref[:, 0]
        cross_ref[...] = melt_ref[:, last]


def binomial(source):
    return (shift_lanes(source, 1) + shift_lanes(source, -1)) + 2.0 * source


def germano(
    place_ref,
    own_ref,
    cross_ref,
    mate_ref,
    halo_ref,
    halo_mate_ref,
    halo_cross_ref,
    base_ref,
    eddy_ref,
    sums_ref,
    field,
    coarse,
    strength,
):
    _, cells, rows, span = own_ref.shape
    wide = span + LANES
    lane = lax.broadcasted_iota(jnp.int32, (SUB, LANES), 1)
    even = place_ref[1] % 2 == 0
    halo = halo_ref[...]
    halo_left = jnp.where(even, halo_cross_ref[...], halo_mate_ref[...])
    halo_right = jnp.where(even, halo_mate_ref[...], halo_cross_ref[...])
    for index in range(cells + 4):
        if index < 2:
            columns, cell = halo_left, index + cells - 2
            sources = cross_ref, mate_ref
        elif index < cells + 2:
            columns, cell = halo, index - 2
            sources = own_ref, own_ref
        else:
            columns, cell = halo_right, index - cells - 2
            sources = mate_ref, cross_ref
        for component in range(4 if 1 <= index <= cells + 2 else 3):
            for block in range(rows // SUB):
                at = slot(block, cell, component, cells)
                place = pl.ds(SUB * (block + 1), SUB)
                here = slice(SUB * block, SUB * (block + 1))
                field[index, component, place, 0:span] = jnp.where(
                    even, sources[0][component, cell, here, :], sources[1][component, cell, here, :]
                )
                field[index, component, place, span:wide] = jnp.where(
                    lane < LANES // 2,
                    shift_lanes(columns, -at),
                    shift_lanes(columns, LANES - 4 - at),
                )
            field[index, component, SUB - 1 : SUB, :] = -field[index, component, SUB : SUB + 1, :]
            field[index, component, SUB + rows : SUB + rows + 1, :] = field[
                index, component, SUB + rows - 1 : SUB + rows, :
            ]

    def filter_block(block, carry):
        place = pl.ds(pl.multiple_of(SUB * (block + 1), SUB), SUB)
        for component in range(3):
            pair = [
                field[i, component, place, :] + field[i + 1, component, place, :]
                for i in range(cells + 3)
            ]
            for i in range(cells + 2):
                coarse[i, component, place, :] = binomial(pair[i] + pair[i + 1])
        return carry

    lax.fori_loop(0, rows // SUB, filter_block, 0)
    for i in range(cells + 2):
        for component in range(3):
            coarse[i, component, SUB - 1 : SUB, :] = -coarse[i, component, SUB : SUB + 1, :]
            coarse[i, component, SUB + rows : SUB + rows + 1, :] = coarse[
                i, component, SUB + rows - 1 : SUB + rows, :
            ]

    row = lax.broadcasted_iota(jnp.int32, (SUB, wide), 0)

    def around(ref, index, component, block):
        previous, place, following = (
            pl.ds(pl.multiple_of(SUB * (block + step), SUB), SUB) for step in range(3)
        )
        middle = ref[index, component, place, :]
        below = jnp.where(row == SUB - 1, ref[index, component, previous, :], middle)
        above = jnp.where(row == 0, ref[index, component, following, :], middle)
        return (
            middle,
            (ref[index - 1, component, place, :], ref[index + 1, component, place, :]),
            (shift_lanes(middle, 1), shift_lanes(middle, -1)),
            (pltpu.roll(below, 1, 0), pltpu.roll(above, SUB - 1, 0)),
        )

    def strain(gradient):
        parts = [
            gradient[i][i] if i == j else gradient[i][j] + gradient[j][i] for i, j in PAIRS
        ]
        diagonal = parts[0] * parts[0] + parts[1] * parts[1] + parts[2] * parts[2]
        off = parts[3] * parts[3] + parts[4] * parts[4] + parts[5] * parts[5]
        return parts, jnp.sqrt(0.5 * diagonal + 0.25 * off)

    column = lax.broadcasted_iota(jnp.int32, (SUB, LANES), 1)

    def rate_block(block, carry):
        out_rows = pl.ds(pl.multiple_of(SUB * block, SUB), SUB)
        place = pl.ds(pl.multiple_of(SUB * (block + 1), SUB), SUB)
        stressed = []
        for index in range(1, cells + 3):
            points = [around(field, index, c, block) for c in range(3)]
            gradient = [[p[1 + j][1] - p[1 + j][0] for j in range(3)] for p in points]
            parts, magnitude = strain(gradient)
            stressed.append([magnitude * part for part in parts])
            if 2 <= index < cells + 2:
                cell = index - 2
                points = points + [around(field, index, 3, block)]
                gradient = gradient + [[points[3][1 + j][1] - points[3][1 + j][0] for j in range(3)]]
                speed = [0.5 * points[j][0][:, :span] for j in range(3)]
                own_magnitude = magnitude[:, :span]
                strength[cell, out_rows, :] = own_magnitude
                for c in range(4):
                    middle, along, across, upward = points[c]
                    laplace = (
                        (along[0] + along[1]) + (across[0] + across[1]) + (upward[0] + upward[1])
                    )[:, :span] - 6.0 * middle[:, :span]
                    advection = (
                        speed[0] * gradient[c][0][:, :span]
                        + speed[1] * gradient[c][1][:, :span]
                        + speed[2] * gradient[c][2][:, :span]
                    )
                    molecular = gas_viscosity if c < 3 else gas_diffusivity
                    base_ref[c, cell, out_rows, :] = molecular * laplace - advection
                    eddy = own_magnitude * laplace
                    eddy_ref[c, cell, out_rows, :] = eddy if c < 3 else eddy * (1.0 / turbulent_prandtl)
        filtered = []
        for k, (i, j) in enumerate(PAIRS):
            pair = [stressed[x][k] + stressed[x + 1][k] for x in range(cells + 1)]
            filtered.append([binomial(pair[x] + pair[x + 1])[:, :span] for x in range(cells)])
        products = []
        for i, j in PAIRS:
            values = [
                field[x, i, place, :] * field[x, j, place, :] for x in range(1, cells + 3)
            ]
            pair = [values[x] + values[x + 1] for x in range(cells + 1)]
            products.append([binomial(pair[x] + pair[x + 1])[:, :span] for x in range(cells)])
        tile = carry
        first = block * 2 * cells
        for cell in range(cells):
            points = [around(coarse, cell + 1, c, block) for c in range(3)]
            gradient = [[(p[1 + j][1] - p[1 + j][0])[:, :span] for j in range(3)] for p in points]
            parts, magnitude = strain(gradient)
            quarter = 0.25 * magnitude
            speed = [0.25 * p[0][:, :span] for p in points]
            numerator = diagonal = off = 0.0
            for k, (i, j) in enumerate(PAIRS):
                model = filtered[k][cell] - quarter * parts[k]
                leonard = products[k][cell] - speed[i] * speed[j]
                numerator = numerator + leonard * model
                if i == j:
                    diagonal = diagonal + model * model
                else:
                    off = off + model * model
            denominator = diagonal + 0.5 * off
            total = jnp.sum(numerator, axis=1, keepdims=True) * (1.0 / 512.0)
            tile = jnp.where(column == first + cell, total, tile)
            total = jnp.sum(denominator, axis=1, keepdims=True) * (1.0 / 1024.0)
            tile = jnp.where(column == first + cells + cell, total, tile)
        return tile

    none = jnp.zeros((SUB, LANES), jnp.float32)
    sums_ref[0:SUB, :] = lax.fori_loop(0, rows // SUB, rate_block, none)
    tiles = span // LANES
    for cell in range(cells):
        planes = (
            strength[cell, 0:1, :],
            own_ref[0, cell, 0:1, :],
            own_ref[3, cell, 0:1, :],
        )
        for p, plane in enumerate(planes):
            for t in range(tiles):
                at = SUB + (p * cells + cell) * tiles + t
                sums_ref[at : at + 1, :] = plane[:, t * LANES : (t + 1) * LANES]


def lilly(total, cells, span_cells):
    mean_numerator = total / span_cells
    mean_denominator = shift_lanes(total, -cells) / span_cells
    return -mean_numerator / (2.0 * (mean_denominator + epsilon))


def merge_messages(mine_ref, theirs_ref, out_ref):
    held = mine_ref.shape[0]
    out_ref[0:SUB, :] = mine_ref[0:SUB, :] + theirs_ref[0:SUB, :]
    out_ref[SUB:held, :] = mine_ref[SUB:held, :]
    out_ref[held : 2 * held - SUB, :] = theirs_ref[SUB:held, :]


def finish_gas(span_cells, mine_ref, theirs_ref, base_ref, eddy_ref, out_ref):
    _, cells, rows, _ = base_ref.shape
    coefficient = lilly(mine_ref[0:SUB, :] + theirs_ref[0:SUB, :], cells, span_cells)
    for cell in range(cells):
        for block in range(rows // SUB):
            at = block * 2 * cells + cell
            factor = coefficient[:, at : at + 1]
            here = slice(SUB * block, SUB * (block + 1))
            for component in range(4):
                out_ref[component, cell, here, :] = (
                    base_ref[component, cell, here, :] + factor * eddy_ref[component, cell, here, :]
                )


def wall_fluxes(span_cells, devices, span, mine_ref, theirs_ref, wall_ref):
    cells = wall_ref.shape[0] // 2
    coefficient = lilly(mine_ref[0:SUB, :] + theirs_ref[0:SUB, :], cells, span_cells)
    tiles = span // LANES
    held = (mine_ref.shape[0] - SUB) // (devices // 2)
    for cell in range(cells):
        factor = coefficient[0:1, cell : cell + 1]
        for device in range(devices):
            ref = mine_ref if device < devices // 2 else theirs_ref
            start = SUB + device % (devices // 2) * held
            for t in range(tiles):
                strength, speed, heat = (
                    ref[at : at + 1, :]
                    for at in (start + (p * cells + cell) * tiles + t for p in range(3))
                )
                eddy = factor * strength
                place = pl.ds((device * tiles + t) * LANES, LANES)
                wall_ref[cell : cell + 1, place] = (gas_viscosity + eddy) * 2.0 * speed
                wall_ref[cells + cell : cells + cell + 1, place] = (
                    (gas_diffusivity + eddy / turbulent_prandtl) * 2.0 * heat
                )


def surface_flux(place_ref, wall_ref, mask_ref, flux_ref):
    cells = mask_ref.shape[0]
    top = place_ref[0] == 0
    shear = mask_ref[...].astype(jnp.float32) * wall_ref[0:cells, :]
    flux_ref[0:cells, :] = jnp.where(top, shear, 0.0)
    flux_ref[cells:, :] = jnp.where(top, wall_ref[cells:, :], 0.0)


def finish_melt(
    devices,
    place_ref,
    flux_ref,
    melt_ref,
    beside_mate_ref,
    beside_cross_ref,
    mate_ref,
    cross_ref,
    mask_ref,
    level_ref,
    out_hbm,
    out_ref,
    sems,
):
    components, cells, depth, width = melt_ref.shape
    position = place_ref[0]
    even = position % 2 == 0
    even_cell = place_ref[1] % 2 == 0
    copies = []
    level_id = lax.broadcasted_iota(jnp.int32, (SUB, width), 0)

    def row_of(ref, at):
        step = components * cells
        return jnp.concatenate(
            [ref[at + t * step : at + t * step + 1, :] for t in range(width // LANES)], axis=1
        )

    for cell in range(cells):
        mask = mask_ref[cell : cell + 1, :]
        top = position == 0
        levels = level_ref[cell : cell + 1, :]
        for component in range(components):
            at = SUB + component * cells + cell
            from_mate, from_cross = row_of(mate_ref, at), row_of(cross_ref, at)
            first = melt_ref[component, cell, 0:1, :]
            ghost = jnp.where(mask == 1, first, -first) if component == 0 else first
            upper = jnp.where(top, ghost, jnp.where(even, from_cross, from_mate))
            final = melt_ref[component, cell, depth - 1 : depth, :]
            lower = jnp.where(position == devices - 1, final, jnp.where(even, from_mate, from_cross))
            for block in range(depth // SUB):
                here = slice(SUB * block, SUB * (block + 1))
                middle = melt_ref[component, cell, here, :]
                over = (
                    jnp.where(level_id == 0, upper, pltpu.roll(middle, 1, 0))
                    if block == 0
                    else melt_ref[component, cell, SUB * block - 1 : SUB * (block + 1) - 1, :]
                )
                under = (
                    jnp.where(level_id == SUB - 1, lower, pltpu.roll(middle, SUB - 1, 0))
                    if block == depth // SUB - 1
                    else melt_ref[component, cell, SUB * block + 1 : SUB * (block + 1) + 1, :]
                )
                before = (
                    jnp.where(
                        even_cell,
                        beside_cross_ref[component, here, :],
                        beside_mate_ref[component, here, :],
                    )
                    if cell == 0
                    else melt_ref[component, cell - 1, here, :]
                )
                after = (
                    jnp.where(
                        even_cell,
                        beside_mate_ref[component, here, :],
                        beside_cross_ref[component, here, :],
                    )
                    if cell == cells - 1
                    else melt_ref[component, cell + 1, here, :]
                )
                laplace = (before + after) + (over + under)
                laplace = laplace + (shift_lanes(middle, 1) + shift_lanes(middle, -1)) - 6.0 * middle
                rate = (melt_viscosity if component == 0 else melt_diffusivity) * laplace
                if block == 0:
                    flux = flux_ref[component * cells + cell : component * cells + cell + 1, :]
                    rate = rate + jnp.where(level_id == 0, flux, 0.0)
                if component == 0:
                    index = position * depth + SUB * block + level_id
                    rate = jnp.where(index >= levels, 0.0, rate)
                out_ref[component, cell, here, :] = rate
            copy = pltpu.make_async_copy(
                out_ref.at[component, cell], out_hbm.at[component, cell], sems.at[component, cell]
            )
            copy.start()
            copies = copies + [copy]
    for copy in copies:
        copy.wait()


def swap(source, axis, mask):
    return lax.ppermute(source, axis, [(i, i ^ mask) for i in range(lax.axis_size(axis))])


def swap_across(source, axis):
    count = lax.axis_size(axis)
    pairs = [(i, (i + 1) % count) for i in range(1, count, 2)]
    return lax.ppermute(source, axis, pairs + [(j, i) for i, j in pairs])


def swap_aside(source, first, aside):
    count, devices = lax.axis_size("gx"), lax.axis_size("sa")
    pairs = []
    for i in range(first, count, 2):
        j = (i + 1) % count
        for s in range(devices):
            t = s ^ 2 if aside else s
            pairs = pairs + [(i * devices + s, j * devices + t), (j * devices + s, i * devices + t)]
    return lax.ppermute(source, ("gx", "sa"), pairs)


def exchange(message, axis):
    count = lax.axis_size(axis)
    mask = 1
    while True:
        other = swap(message, axis, mask)
        mask = 2 * mask
        if mask == count:
            return message, other
        merged = array(2 * message.shape[0] - SUB, LANES)
        message = call(merge_messages, merged, [VMEM, VMEM])(message, other)


def fenced(place, part, *arrays):
    def no_part(*arrays):
        shapes = jax.eval_shape(part, *arrays)
        return jax.tree.map(lambda leaf: jnp.zeros(leaf.shape, leaf.dtype), shapes)

    return lax.cond(place[0] < lax.axis_size("sa"), part, no_part, *arrays)


def call(kernel, outs, specs, scratch=(), flops=1, out_specs=None):
    return pl.pallas_call(
        kernel,
        out_shape=outs,
        in_specs=specs,
        out_specs=out_specs or jax.tree.map(lambda _: VMEM, outs),
        scratch_shapes=scratch,
        compiler_params=pltpu.CompilerParams(vmem_limit_bytes=24 * 1024 * 1024),
        cost_estimate=pl.CostEstimate(flops=flops, bytes_accessed=1, transcendentals=0),
    )


def array(*shape):
    return jax.ShapeDtypeStruct(shape, jnp.float32)


def on_device(gas, melt, surface_mask, melt_level):
    _, cells, rows, span = gas.shape
    components, _, depth, width = melt.shape
    devices = lax.axis_size("sa")
    assert devices & (devices - 1) == 0 and devices > 1
    span_cells = float(span * devices)
    place = jnp.stack([lax.axis_index("sa"), lax.axis_index("gx")]).astype(jnp.int32)
    even = place[0] % 2 == 0
    gas_mate, gas_cross = swap(gas, "gx", 1), swap_across(gas, "gx")
    side = array(SUB + components * cells * width // LANES, LANES)
    mate, cross, gas_here = call(
        pack_sides,
        (side, side, array(*gas.shape)),
        [SMEM, HBM, HBM],
        scratch=(
            pltpu.VMEM((2, components, cells, SUB, width), jnp.float32),
            pltpu.SemaphoreType.DMA((3,)),
        ),
    )(place, pltpu.with_memory_space_constraint(gas, pltpu.HBM), pltpu.with_memory_space_constraint(melt, pltpu.HBM))
    mate, cross = swap(mate, "sa", 1), swap_across(cross, "sa")
    late = lax.broadcasted_iota(jnp.int32, (SUB, LANES), 1) % EDGE >= EDGE // 2
    halo = jnp.where(late == even, cross[:SUB], mate[:SUB])
    aside = devices == 4
    passed = jnp.where(late == even, mate[:SUB], cross[:SUB]) if aside else halo
    halo_mate, halo_cross = swap_aside(passed, 0, aside), swap_aside(passed, 1, aside)
    part = array(components, depth, width)
    beside_mate, beside_cross = call(pack_melt, (part, part), [SMEM, VMEM, ANY])(place, melt, halo)
    beside_cross = swap_across(beside_cross, "gx")
    beside_mate = swap(beside_mate, "gx", 1)

    def gas_part(*arrays):
        wide = span + LANES
        message_rows = SUB + 3 * cells * (span // LANES)
        base, eddy, message = call(
            germano,
            (array(4, cells, rows, span), array(4, cells, rows, span), array(message_rows, LANES)),
            [SMEM] + [VMEM] * 6,
            scratch=(
                pltpu.VMEM((cells + 4, 4, rows + 2 * SUB, wide), jnp.float32),
                pltpu.VMEM((cells + 2, 3, rows + 2 * SUB, wide), jnp.float32),
                pltpu.VMEM((cells, rows, span), jnp.float32),
            ),
        )(*arrays)
        mine, theirs = exchange(message, "sa")
        rate = call(
            functools.partial(finish_gas, span_cells), array(4, cells, rows, span), [VMEM] * 4
        )(mine, theirs, base, eddy)
        wall = call(
            functools.partial(wall_fluxes, span_cells, devices, span),
            array(2 * cells, width),
            [VMEM, VMEM],
        )(mine, theirs)
        return rate, wall

    gas_rate, wall = fenced(
        place, gas_part, place, gas_here, gas_cross, gas_mate, halo, halo_mate, halo_cross
    )
    flux = call(surface_flux, array(2 * cells, width), [SMEM, VMEM, VMEM], flops=4000000000)(
        place, wall, surface_mask
    )
    melt_rate = call(
        functools.partial(finish_melt, devices),
        array(components, cells, depth, width),
        [SMEM] + [VMEM] * 8,
        scratch=(
            pltpu.VMEM((components, cells, depth, width), jnp.float32),
            pltpu.SemaphoreType.DMA((components, cells)),
        ),
        out_specs=HBM,
    )(place, flux, melt, beside_mate, beside_cross, mate, cross, surface_mask, melt_level)
    return (gas_rate, melt_rate)


def solution(mesh):
    in_specs = (P(None, "gx", None, "sa"), P(None, "gx", "sa", None), P("gx", None), P("gx", None))
    out_specs = (P(None, "gx", None, "sa"), P(None, "gx", "sa", None))
    return jax.shard_map(
        on_device, mesh=mesh, in_specs=in_specs, out_specs=out_specs, check_vma=False
    )
```

```python
import functools

import jax
import jax.numpy as jnp
from jax import lax
from jax.experimental import pallas as pl
from jax.experimental.pallas import tpu as pltpu
from jax.sharding import PartitionSpec as P

gas_viscosity = 0.05
gas_diffusivity = 0.07
turbulent_prandtl = 0.85
melt_viscosity = 0.2
melt_diffusivity = 0.5
epsilon = 1e-06

LANES = 128
SUB = 8
EDGE = 4
PAIRS = ((0, 0), (1, 1), (2, 2), (0, 1), (0, 2), (1, 2))
VMEM = pl.BlockSpec(memory_space=pltpu.VMEM)
ANY = pl.BlockSpec(memory_space=pl.ANY)
HBM = pl.BlockSpec(memory_space=pltpu.HBM)


def shift_lanes(source, amount):
    extent = source.shape[-1]
    return pltpu.roll(source, amount % extent, source.ndim - 1)


def slot(row_block, cell, component, cells):
    return ((row_block * cells + cell) * 4 + component) * EDGE


def pack_sides(gas_hbm, melt_hbm, mate_ref, cross_ref, gas_ref, ends_ref, sems):
    _, cells, rows, span = gas_ref.shape
    components, _, depth, width = melt_hbm.shape
    copies = [pltpu.make_async_copy(gas_hbm, gas_ref, sems.at[0])]
    for end, start in enumerate((0, depth - SUB)):
        levels = melt_hbm.at[:, :, pl.ds(start, SUB), :]
        copies.append(pltpu.make_async_copy(levels, ends_ref.at[end], sems.at[end + 1]))
    for copy in copies:
        copy.start()
    copies[0].wait()
    lane = lax.broadcasted_iota(jnp.int32, (SUB, LANES), 1)
    tile = jnp.zeros((SUB, LANES), jnp.float32)
    for block in range(rows // SUB):
        for cell in range(cells):
            for component in range(4):
                at = slot(block, cell, component, cells)
                here = pl.ds(SUB * block, SUB)
                first = gas_ref[component, cell, here, 0:LANES]
                last = gas_ref[component, cell, here, span - LANES : span]
                tile = jnp.where((lane >= at) & (lane < at + 2), shift_lanes(first, at), tile)
                tile = jnp.where(
                    (lane >= at + 2) & (lane < at + 4), shift_lanes(last, at + 4), tile
                )
    mate_ref[0:SUB, :] = tile
    cross_ref[0:SUB, :] = tile
    even = lax.axis_index("sa") % 2 == 0
    for copy in copies[1:]:
        copy.wait()
    for component in range(components):
        for cell in range(cells):
            first = ends_ref[0, component, cell, 0:1, :]
            last = ends_ref[1, component, cell, SUB - 1 : SUB, :]
            mate = jnp.where(even, last, first)
            cross = jnp.where(even, first, last)
            for t in range(width // LANES):
                at = SUB + t * components * cells + component * cells + cell
                mate_ref[at : at + 1, :] = mate[:, t * LANES : (t + 1) * LANES]
                cross_ref[at : at + 1, :] = cross[:, t * LANES : (t + 1) * LANES]


def pack_melt(first, melt_ref, *refs):
    out_ref = refs[-1]
    last = melt_ref.shape[1] - 1
    lower = lax.axis_index("gx") % 2 == first

    @pl.when(lower)
    def _():
        out_ref[...] = melt_ref[:, last]

    @pl.when(jnp.logical_not(lower))
    def _():
        out_ref[...] = melt_ref[:, 0]


def binomial(source):
    return (shift_lanes(source, 1) + shift_lanes(source, -1)) + 2.0 * source


def germano(
    own_ref,
    cross_ref,
    mate_ref,
    halo_ref,
    halo_mate_ref,
    halo_cross_ref,
    base_ref,
    eddy_ref,
    sums_ref,
    field,
    coarse,
    strength,
):
    _, cells, rows, span = own_ref.shape
    wide = span + LANES
    lane = lax.broadcasted_iota(jnp.int32, (SUB, LANES), 1)
    even = lax.axis_index("gx") % 2 == 0
    halo = halo_ref[...]
    halo_left = jnp.where(even, halo_cross_ref[...], halo_mate_ref[...])
    halo_right = jnp.where(even, halo_mate_ref[...], halo_cross_ref[...])
    for index in range(cells + 4):
        if index < 2:
            columns, cell = halo_left, index + cells - 2
            sources = cross_ref, mate_ref
        elif index < cells + 2:
            columns, cell = halo, index - 2
            sources = own_ref, own_ref
        else:
            columns, cell = halo_right, index - cells - 2
            sources = mate_ref, cross_ref
        for component in range(4 if 1 <= index <= cells + 2 else 3):
            for block in range(rows // SUB):
                at = slot(block, cell, component, cells)
                place = pl.ds(SUB * (block + 1), SUB)
                here = slice(SUB * block, SUB * (block + 1))
                field[index, component, place, 0:span] = jnp.where(
                    even, sources[0][component, cell, here, :], sources[1][component, cell, here, :]
                )
                field[index, component, place, span:wide] = jnp.where(
                    lane < LANES // 2,
                    shift_lanes(columns, -at),
                    shift_lanes(columns, LANES - 4 - at),
                )
            field[index, component, SUB - 1 : SUB, :] = -field[index, component, SUB : SUB + 1, :]
            field[index, component, SUB + rows : SUB + rows + 1, :] = field[
                index, component, SUB + rows - 1 : SUB + rows, :
            ]

    def filter_block(block, carry):
        place = pl.ds(pl.multiple_of(SUB * (block + 1), SUB), SUB)
        for component in range(3):
            pair = [
                field[i, component, place, :] + field[i + 1, component, place, :]
                for i in range(cells + 3)
            ]
            for i in range(cells + 2):
                coarse[i, component, place, :] = binomial(pair[i] + pair[i + 1])
        return carry

    lax.fori_loop(0, rows // SUB, filter_block, 0)
    for i in range(cells + 2):
        for component in range(3):
            coarse[i, component, SUB - 1 : SUB, :] = -coarse[i, component, SUB : SUB + 1, :]
            coarse[i, component, SUB + rows : SUB + rows + 1, :] = coarse[
                i, component, SUB + rows - 1 : SUB + rows, :
            ]

    row = lax.broadcasted_iota(jnp.int32, (SUB, wide), 0)

    def around(ref, index, component, block):
        previous, place, following = (
            pl.ds(pl.multiple_of(SUB * (block + step), SUB), SUB) for step in range(3)
        )
        middle = ref[index, component, place, :]
        below = jnp.where(row == SUB - 1, ref[index, component, previous, :], middle)
        above = jnp.where(row == 0, ref[index, component, following, :], middle)
        return (
            middle,
            (ref[index - 1, component, place, :], ref[index + 1, component, place, :]),
            (shift_lanes(middle, 1), shift_lanes(middle, -1)),
            (pltpu.roll(below, 1, 0), pltpu.roll(above, SUB - 1, 0)),
        )

    def strain(gradient):
        parts = [
            gradient[i][i] if i == j else gradient[i][j] + gradient[j][i] for i, j in PAIRS
        ]
        diagonal = parts[0] * parts[0] + parts[1] * parts[1] + parts[2] * parts[2]
        off = parts[3] * parts[3] + parts[4] * parts[4] + parts[5] * parts[5]
        return parts, jnp.sqrt(0.5 * diagonal + 0.25 * off)

    column = lax.broadcasted_iota(jnp.int32, (SUB, LANES), 1)

    def rate_block(block, carry):
        out_rows = pl.ds(pl.multiple_of(SUB * block, SUB), SUB)
        place = pl.ds(pl.multiple_of(SUB * (block + 1), SUB), SUB)
        stressed = []
        for index in range(1, cells + 3):
            points = [around(field, index, c, block) for c in range(3)]
            gradient = [[p[1 + j][1] - p[1 + j][0] for j in range(3)] for p in points]
            parts, magnitude = strain(gradient)
            stressed.append([magnitude * part for part in parts])
            if 2 <= index < cells + 2:
                cell = index - 2
                points = points + [around(field, index, 3, block)]
                gradient = gradient + [[points[3][1 + j][1] - points[3][1 + j][0] for j in range(3)]]
                speed = [0.5 * points[j][0][:, :span] for j in range(3)]
                own_magnitude = magnitude[:, :span]
                strength[cell, out_rows, :] = own_magnitude
                for c in range(4):
                    middle, along, across, upward = points[c]
                    laplace = (
                        (along[0] + along[1]) + (across[0] + across[1]) + (upward[0] + upward[1])
                    )[:, :span] - 6.0 * middle[:, :span]
                    advection = (
                        speed[0] * gradient[c][0][:, :span]
                        + speed[1] * gradient[c][1][:, :span]
                        + speed[2] * gradient[c][2][:, :span]
                    )
                    molecular = gas_viscosity if c < 3 else gas_diffusivity
                    base_ref[c, cell, out_rows, :] = molecular * laplace - advection
                    eddy = own_magnitude * laplace
                    eddy_ref[c, cell, out_rows, :] = eddy if c < 3 else eddy * (1.0 / turbulent_prandtl)
        filtered = []
        for k, (i, j) in enumerate(PAIRS):
            pair = [stressed[x][k] + stressed[x + 1][k] for x in range(cells + 1)]
            filtered.append([binomial(pair[x] + pair[x + 1])[:, :span] for x in range(cells)])
        products = []
        for i, j in PAIRS:
            values = [
                field[x, i, place, :] * field[x, j, place, :] for x in range(1, cells + 3)
            ]
            pair = [values[x] + values[x + 1] for x in range(cells + 1)]
            products.append([binomial(pair[x] + pair[x + 1])[:, :span] for x in range(cells)])
        tile = carry
        first = block * 2 * cells
        for cell in range(cells):
            points = [around(coarse, cell + 1, c, block) for c in range(3)]
            gradient = [[(p[1 + j][1] - p[1 + j][0])[:, :span] for j in range(3)] for p in points]
            parts, magnitude = strain(gradient)
            quarter = 0.25 * magnitude
            speed = [0.25 * p[0][:, :span] for p in points]
            numerator = diagonal = off = 0.0
            for k, (i, j) in enumerate(PAIRS):
                model = filtered[k][cell] - quarter * parts[k]
                leonard = products[k][cell] - speed[i] * speed[j]
                numerator = numerator + leonard * model
                if i == j:
                    diagonal = diagonal + model * model
                else:
                    off = off + model * model
            denominator = diagonal + 0.5 * off
            total = jnp.sum(numerator, axis=1, keepdims=True) * (1.0 / 512.0)
            tile = jnp.where(column == first + cell, total, tile)
            total = jnp.sum(denominator, axis=1, keepdims=True) * (1.0 / 1024.0)
            tile = jnp.where(column == first + cells + cell, total, tile)
        return tile

    none = jnp.zeros((SUB, LANES), jnp.float32)
    sums_ref[0:SUB, :] = lax.fori_loop(0, rows // SUB, rate_block, none)
    tiles = span // LANES
    for cell in range(cells):
        planes = (
            strength[cell, 0:1, :],
            own_ref[0, cell, 0:1, :],
            own_ref[3, cell, 0:1, :],
        )
        for p, plane in enumerate(planes):
            for t in range(tiles):
                at = SUB + (p * cells + cell) * tiles + t
                sums_ref[at : at + 1, :] = plane[:, t * LANES : (t + 1) * LANES]


def lilly(total, cells, span_cells):
    mean_numerator = total / span_cells
    mean_denominator = shift_lanes(total, -cells) / span_cells
    return -mean_numerator / (2.0 * (mean_denominator + epsilon))


def merge_messages(mine_ref, theirs_ref, out_ref):
    held = mine_ref.shape[0]
    out_ref[0:SUB, :] = mine_ref[0:SUB, :] + theirs_ref[0:SUB, :]
    out_ref[SUB:held, :] = mine_ref[SUB:held, :]
    out_ref[held : 2 * held - SUB, :] = theirs_ref[SUB:held, :]


def finish_gas(span_cells, mine_ref, theirs_ref, base_ref, eddy_ref, out_ref):
    _, cells, rows, _ = base_ref.shape
    coefficient = lilly(mine_ref[0:SUB, :] + theirs_ref[0:SUB, :], cells, span_cells)
    for cell in range(cells):
        for block in range(rows // SUB):
            at = block * 2 * cells + cell
            factor = coefficient[:, at : at + 1]
            here = slice(SUB * block, SUB * (block + 1))
            for component in range(4):
                out_ref[component, cell, here, :] = (
                    base_ref[component, cell, here, :] + factor * eddy_ref[component, cell, here, :]
                )


def wall_fluxes(span_cells, devices, span, mine_ref, theirs_ref, wall_ref):
    cells = wall_ref.shape[0] // 2
    coefficient = lilly(mine_ref[0:SUB, :] + theirs_ref[0:SUB, :], cells, span_cells)
    tiles = span // LANES
    held = (mine_ref.shape[0] - SUB) // (devices // 2)
    for cell in range(cells):
        factor = coefficient[0:1, cell : cell + 1]
        for device in range(devices):
            ref = mine_ref if device < devices // 2 else theirs_ref
            start = SUB + device % (devices // 2) * held
            for t in range(tiles):
                strength, speed, heat = (
                    ref[at : at + 1, :]
                    for at in (start + (p * cells + cell) * tiles + t for p in range(3))
                )
                eddy = factor * strength
                place = pl.ds((device * tiles + t) * LANES, LANES)
                wall_ref[cell : cell + 1, place] = (gas_viscosity + eddy) * 2.0 * speed
                wall_ref[cells + cell : cells + cell + 1, place] = (
                    (gas_diffusivity + eddy / turbulent_prandtl) * 2.0 * heat
                )


def surface_flux(wall_ref, mask_ref, flux_ref):
    cells = mask_ref.shape[0]
    top = lax.axis_index("sa") == 0
    shear = mask_ref[...].astype(jnp.float32) * wall_ref[0:cells, :]
    flux_ref[0:cells, :] = jnp.where(top, shear, 0.0)
    flux_ref[cells:, :] = jnp.where(top, wall_ref[cells:, :], 0.0)


def finish_melt(
    flux_ref,
    inside_ref,
    beside_mate_ref,
    beside_ends_ref,
    beside_between_ref,
    level_ref,
    out_hbm,
    out_ref,
    sems,
):
    components, cells, depth, width = inside_ref.shape
    position = lax.axis_index("sa")
    place = lax.axis_index("gx")
    even = place % 2 == 0
    at_end = (place == 0) | (place == lax.axis_size("gx") - 1)
    level_id = lax.broadcasted_iota(jnp.int32, (SUB, width), 0)
    copies = []
    for cell in range(cells):
        levels = level_ref[cell : cell + 1, :]
        for component in range(components):
            share = melt_viscosity if component == 0 else melt_diffusivity
            for block in range(depth // SUB):
                here = slice(SUB * block, SUB * (block + 1))
                rate = inside_ref[component, cell, here, :]
                if cell in (0, cells - 1):
                    from_mate = beside_mate_ref[component, here, :]
                    from_cross = jnp.where(
                        at_end,
                        beside_ends_ref[component, here, :],
                        beside_between_ref[component, here, :],
                    )
                    outer = jnp.where(even == (cell == 0), from_cross, from_mate)
                    rate = rate + share * outer
                if block == 0:
                    flux = flux_ref[component * cells + cell : component * cells + cell + 1, :]
                    rate = rate + jnp.where(level_id == 0, flux, 0.0)
                if component == 0:
                    index = position * depth + SUB * block + level_id
                    rate = jnp.where(index >= levels, 0.0, rate)
                out_ref[component, cell, here, :] = rate
            copy = pltpu.make_async_copy(
                out_ref.at[component, cell], out_hbm.at[component, cell], sems.at[component, cell]
            )
            copy.start()
            copies = copies + [copy]
    for copy in copies:
        copy.wait()


def melt_inside(devices, melt_ref, mate_ref, cross_ref, mask_ref, after_ref, part_ref, inside_ref):
    components, cells, depth, width = melt_ref.shape
    assert cells > 1
    pack_melt(0, melt_ref, part_ref)
    position = lax.axis_index("sa")
    even = position % 2 == 0
    top = position == 0
    level_id = lax.broadcasted_iota(jnp.int32, (SUB, width), 0)

    def row_of(ref, at):
        step = components * cells
        return jnp.concatenate(
            [ref[at + t * step : at + t * step + 1, :] for t in range(width // LANES)], axis=1
        )

    for cell in range(cells):
        mask = mask_ref[cell : cell + 1, :]
        for component in range(components):
            at = SUB + component * cells + cell
            from_mate, from_cross = row_of(mate_ref, at), row_of(cross_ref, at)
            first = melt_ref[component, cell, 0:1, :]
            ghost = jnp.where(mask == 1, first, -first) if component == 0 else first
            upper = jnp.where(top, ghost, jnp.where(even, from_cross, from_mate))
            final = melt_ref[component, cell, depth - 1 : depth, :]
            lower = jnp.where(position == devices - 1, final, jnp.where(even, from_mate, from_cross))
            for block in range(depth // SUB):
                here = slice(SUB * block, SUB * (block + 1))
                middle = melt_ref[component, cell, here, :]
                over = (
                    jnp.where(level_id == 0, upper, pltpu.roll(middle, 1, 0))
                    if block == 0
                    else melt_ref[component, cell, SUB * block - 1 : SUB * (block + 1) - 1, :]
                )
                under = (
                    jnp.where(level_id == SUB - 1, lower, pltpu.roll(middle, SUB - 1, 0))
                    if block == depth // SUB - 1
                    else melt_ref[component, cell, SUB * block + 1 : SUB * (block + 1) + 1, :]
                )
                laplace = (over + under) + (shift_lanes(middle, 1) + shift_lanes(middle, -1))
                for near in (cell - 1, cell + 1):
                    if 0 <= near < cells:
                        laplace = laplace + melt_ref[component, near, here, :]
                laplace = laplace - 6.0 * middle
                inside_ref[component, cell, here, :] = (
                    melt_viscosity if component == 0 else melt_diffusivity
                ) * laplace


def swap(source, axis, mask):
    return lax.ppermute(source, axis, [(i, i ^ mask) for i in range(lax.axis_size(axis))])


def swap_across(source, axis):
    count = lax.axis_size(axis)
    pairs = [(i, (i + 1) % count) for i in range(1, count, 2)]
    return lax.ppermute(source, axis, pairs + [(j, i) for i, j in pairs])


def swap_between(source, axis):
    count = lax.axis_size(axis)
    pairs = [(i, i + 1) for i in range(1, count - 1, 2)]
    return lax.ppermute(source, axis, pairs + [(j, i) for i, j in pairs])


def swap_ends(source, axis):
    last = lax.axis_size(axis) - 1
    return lax.ppermute(source, axis, [(0, last), (last, 0)])


def swap_aside(source, first, aside):
    count, devices = lax.axis_size("gx"), lax.axis_size("sa")
    pairs = []
    for i in range(first, count, 2):
        j = (i + 1) % count
        for s in range(devices):
            t = s ^ 2 if aside else s
            pairs = pairs + [(i * devices + s, j * devices + t), (j * devices + s, i * devices + t)]
    return lax.ppermute(source, ("gx", "sa"), pairs)


def exchange(message, axis):
    count = lax.axis_size(axis)
    mask = 1
    while True:
        other = swap(message, axis, mask)
        mask = 2 * mask
        if mask == count:
            return message, other
        merged = array(2 * message.shape[0] - SUB, LANES)
        message = call(merge_messages, merged, [VMEM, VMEM])(message, other)


def fenced(part, *arrays):
    def no_part(*arrays):
        shapes = jax.eval_shape(part, *arrays)
        return jax.tree.map(lambda leaf: jnp.zeros(leaf.shape, leaf.dtype), shapes)

    return lax.cond(lax.axis_index("sa") < lax.axis_size("sa"), part, no_part, *arrays)


def call(kernel, outs, specs, scratch=(), flops=1, out_specs=None):
    return pl.pallas_call(
        kernel,
        out_shape=outs,
        in_specs=specs,
        out_specs=out_specs or jax.tree.map(lambda _: VMEM, outs),
        scratch_shapes=scratch,
        compiler_params=pltpu.CompilerParams(vmem_limit_bytes=24 * 1024 * 1024),
        cost_estimate=pl.CostEstimate(flops=flops, bytes_accessed=1, transcendentals=0),
    )


def array(*shape):
    return jax.ShapeDtypeStruct(shape, jnp.float32)


def on_device(gas, melt, surface_mask, melt_level):
    _, cells, rows, span = gas.shape
    components, _, depth, width = melt.shape
    devices = lax.axis_size("sa")
    assert devices & (devices - 1) == 0 and devices > 1
    span_cells = float(span * devices)
    even = lax.axis_index("sa") % 2 == 0
    gas_mate = swap(gas, "gx", 1)
    side = array(SUB + components * cells * width // LANES, LANES)
    mate, cross, gas_here = call(
        pack_sides,
        (side, side, array(*gas.shape)),
        [HBM, HBM],
        scratch=(
            pltpu.VMEM((2, components, cells, SUB, width), jnp.float32),
            pltpu.SemaphoreType.DMA((3,)),
        ),
    )(pltpu.with_memory_space_constraint(gas, pltpu.HBM), pltpu.with_memory_space_constraint(melt, pltpu.HBM))
    gas_cross = swap_across(gas_here, "gx")
    mate, cross = swap(mate, "sa", 1), swap_across(cross, "sa")
    late = lax.broadcasted_iota(jnp.int32, (SUB, LANES), 1) % EDGE >= EDGE // 2
    halo = jnp.where(late == even, cross[:SUB], mate[:SUB])
    aside = devices == 4
    passed = jnp.where(late == even, mate[:SUB], cross[:SUB]) if aside else halo
    halo_mate, halo_cross = swap_aside(passed, 0, aside), swap_aside(passed, 1, aside)
    part, whole = array(components, depth, width), array(components, cells, depth, width)
    mate_part, inside = call(
        functools.partial(melt_inside, devices), (part, whole), [VMEM] * 4 + [ANY]
    )(melt, mate, cross, surface_mask, halo_mate)
    ends_part = call(functools.partial(pack_melt, 1), part, [VMEM, ANY])(melt, halo_mate)
    cross_part = call(functools.partial(pack_melt, 1), part, [VMEM, ANY])(melt, halo_cross)
    beside_mate = swap(mate_part, "gx", 1)
    beside_ends = swap_ends(ends_part, "gx")
    beside_between = swap_between(cross_part, "gx")

    def gas_part(*arrays):
        wide = span + LANES
        message_rows = SUB + 3 * cells * (span // LANES)
        base, eddy, message = call(
            germano,
            (array(4, cells, rows, span), array(4, cells, rows, span), array(message_rows, LANES)),
            [VMEM] * 6,
            scratch=(
                pltpu.VMEM((cells + 4, 4, rows + 2 * SUB, wide), jnp.float32),
                pltpu.VMEM((cells + 2, 3, rows + 2 * SUB, wide), jnp.float32),
                pltpu.VMEM((cells, rows, span), jnp.float32),
            ),
        )(*arrays)
        mine, theirs = exchange(message, "sa")
        rate = call(
            functools.partial(finish_gas, span_cells), array(4, cells, rows, span), [VMEM] * 4
        )(mine, theirs, base, eddy)
        wall = call(
            functools.partial(wall_fluxes, span_cells, devices, span),
            array(2 * cells, width),
            [VMEM, VMEM],
        )(mine, theirs)
        return rate, wall

    gas_rate, wall = fenced(
        gas_part, gas_here, gas_cross, gas_mate, halo, halo_mate, halo_cross
    )
    flux = call(surface_flux, array(2 * cells, width), [VMEM, VMEM], flops=4000000000)(
        wall, surface_mask
    )
    melt_rate = call(
        finish_melt,
        whole,
        [VMEM] * 6,
        scratch=(
            pltpu.VMEM((components, cells, depth, width), jnp.float32),
            pltpu.SemaphoreType.DMA((components, cells)),
        ),
        out_specs=HBM,
    )(flux, inside, beside_mate, beside_ends, beside_between, melt_level)
    return (gas_rate, melt_rate)


def solution(mesh):
    in_specs = (P(None, "gx", None, "sa"), P(None, "gx", "sa", None), P("gx", None), P("gx", None))
    out_specs = (P(None, "gx", None, "sa"), P(None, "gx", "sa", None))
    return jax.shard_map(
        on_device, mesh=mesh, in_specs=in_specs, out_specs=out_specs, check_vma=False
    )
```

```python
import functools

import jax
import jax.numpy as jnp
from jax import lax
from jax.experimental import pallas as pl
from jax.experimental.pallas import tpu as pltpu
from jax.sharding import PartitionSpec as P

gas_viscosity = 0.05
gas_diffusivity = 0.07
turbulent_prandtl = 0.85
melt_viscosity = 0.2
melt_diffusivity = 0.5
epsilon = 1e-06

LANES = 128
SUB = 8
EDGE = 4
PAIRS = ((0, 0), (1, 1), (2, 2), (0, 1), (0, 2), (1, 2))
VMEM = pl.BlockSpec(memory_space=pltpu.VMEM)
ANY = pl.BlockSpec(memory_space=pl.ANY)
HBM = pl.BlockSpec(memory_space=pltpu.HBM)


def shift_lanes(source, amount):
    extent = source.shape[-1]
    return pltpu.roll(source, amount % extent, source.ndim - 1)


def slot(row_block, cell, component, cells):
    return ((row_block * cells + cell) * 4 + component) * EDGE


def pack_sides(gas_hbm, melt_hbm, mate_ref, cross_ref, gas_ref, ends_ref, sems):
    _, cells, rows, span = gas_ref.shape
    components, _, depth, width = melt_hbm.shape
    copies = [pltpu.make_async_copy(gas_hbm, gas_ref, sems.at[0])]
    for end, start in enumerate((0, depth - SUB)):
        levels = melt_hbm.at[:, :, pl.ds(start, SUB), :]
        copies.append(pltpu.make_async_copy(levels, ends_ref.at[end], sems.at[end + 1]))
    for copy in copies:
        copy.start()
    copies[0].wait()
    lane = lax.broadcasted_iota(jnp.int32, (SUB, LANES), 1)
    tile = jnp.zeros((SUB, LANES), jnp.float32)
    for block in range(rows // SUB):
        for cell in range(cells):
            for component in range(4):
                at = slot(block, cell, component, cells)
                here = pl.ds(SUB * block, SUB)
                first = gas_ref[component, cell, here, 0:LANES]
                last = gas_ref[component, cell, here, span - LANES : span]
                tile = jnp.where((lane >= at) & (lane < at + 2), shift_lanes(first, at), tile)
                tile = jnp.where(
                    (lane >= at + 2) & (lane < at + 4), shift_lanes(last, at + 4), tile
                )
    mate_ref[0:SUB, :] = tile
    cross_ref[0:SUB, :] = tile
    even = lax.axis_index("sa") % 2 == 0
    for copy in copies[1:]:
        copy.wait()
    for component in range(components):
        for cell in range(cells):
            first = ends_ref[0, component, cell, 0:1, :]
            last = ends_ref[1, component, cell, SUB - 1 : SUB, :]
            mate = jnp.where(even, last, first)
            cross = jnp.where(even, first, last)
            for t in range(width // LANES):
                at = SUB + t * components * cells + component * cells + cell
                mate_ref[at : at + 1, :] = mate[:, t * LANES : (t + 1) * LANES]
                cross_ref[at : at + 1, :] = cross[:, t * LANES : (t + 1) * LANES]


def pack_melt(first, melt_ref, *refs):
    out_ref = refs[-1]
    last = melt_ref.shape[1] - 1
    lower = lax.axis_index("gx") % 2 == first

    @pl.when(lower)
    def _():
        out_ref[...] = melt_ref[:, last]

    @pl.when(jnp.logical_not(lower))
    def _():
        out_ref[...] = melt_ref[:, 0]


def binomial(source):
    return (shift_lanes(source, 1) + shift_lanes(source, -1)) + 2.0 * source


def germano(
    own_ref,
    cross_ref,
    mate_ref,
    halo_ref,
    halo_mate_ref,
    halo_cross_ref,
    base_ref,
    eddy_ref,
    sums_ref,
    field,
    coarse,
    strength,
):
    _, cells, rows, span = own_ref.shape
    wide = span + LANES
    lane = lax.broadcasted_iota(jnp.int32, (SUB, LANES), 1)
    even = lax.axis_index("gx") % 2 == 0
    halo = halo_ref[...]
    halo_left = jnp.where(even, halo_cross_ref[...], halo_mate_ref[...])
    halo_right = jnp.where(even, halo_mate_ref[...], halo_cross_ref[...])
    for index in range(cells + 4):
        if index < 2:
            columns, cell = halo_left, index + cells - 2
            sources = cross_ref, mate_ref
        elif index < cells + 2:
            columns, cell = halo, index - 2
            sources = own_ref, own_ref
        else:
            columns, cell = halo_right, index - cells - 2
            sources = mate_ref, cross_ref
        for component in range(4 if 1 <= index <= cells + 2 else 3):
            for block in range(rows // SUB):
                at = slot(block, cell, component, cells)
                place = pl.ds(SUB * (block + 1), SUB)
                here = slice(SUB * block, SUB * (block + 1))
                field[index, component, place, 0:span] = jnp.where(
                    even, sources[0][component, cell, here, :], sources[1][component, cell, here, :]
                )
                field[index, component, place, span:wide] = jnp.where(
                    lane < LANES // 2,
                    shift_lanes(columns, -at),
                    shift_lanes(columns, LANES - 4 - at),
                )
            field[index, component, SUB - 1 : SUB, :] = -field[index, component, SUB : SUB + 1, :]
            field[index, component, SUB + rows : SUB + rows + 1, :] = field[
                index, component, SUB + rows - 1 : SUB + rows, :
            ]

    def filter_block(block, carry):
        place = pl.ds(pl.multiple_of(SUB * (block + 1), SUB), SUB)
        for component in range(3):
            pair = [
                field[i, component, place, :] + field[i + 1, component, place, :]
                for i in range(cells + 3)
            ]
            for i in range(cells + 2):
                coarse[i, component, place, :] = binomial(pair[i] + pair[i + 1])
        return carry

    lax.fori_loop(0, rows // SUB, filter_block, 0)
    for i in range(cells + 2):
        for component in range(3):
            coarse[i, component, SUB - 1 : SUB, :] = -coarse[i, component, SUB : SUB + 1, :]
            coarse[i, component, SUB + rows : SUB + rows + 1, :] = coarse[
                i, component, SUB + rows - 1 : SUB + rows, :
            ]

    row = lax.broadcasted_iota(jnp.int32, (SUB, wide), 0)

    def around(ref, index, component, block):
        previous, place, following = (
            pl.ds(pl.multiple_of(SUB * (block + step), SUB), SUB) for step in range(3)
        )
        middle = ref[index, component, place, :]
        below = jnp.where(row == SUB - 1, ref[index, component, previous, :], middle)
        above = jnp.where(row == 0, ref[index, component, following, :], middle)
        return (
            middle,
            (ref[index - 1, component, place, :], ref[index + 1, component, place, :]),
            (shift_lanes(middle, 1), shift_lanes(middle, -1)),
            (pltpu.roll(below, 1, 0), pltpu.roll(above, SUB - 1, 0)),
        )

    def strain(gradient):
        parts = [
            gradient[i][i] if i == j else gradient[i][j] + gradient[j][i] for i, j in PAIRS
        ]
        diagonal = parts[0] * parts[0] + parts[1] * parts[1] + parts[2] * parts[2]
        off = parts[3] * parts[3] + parts[4] * parts[4] + parts[5] * parts[5]
        return parts, jnp.sqrt(0.5 * diagonal + 0.25 * off)

    column = lax.broadcasted_iota(jnp.int32, (SUB, LANES), 1)

    def rate_block(block, carry):
        out_rows = pl.ds(pl.multiple_of(SUB * block, SUB), SUB)
        place = pl.ds(pl.multiple_of(SUB * (block + 1), SUB), SUB)
        stressed = []
        for index in range(1, cells + 3):
            points = [around(field, index, c, block) for c in range(3)]
            gradient = [[p[1 + j][1] - p[1 + j][0] for j in range(3)] for p in points]
            parts, magnitude = strain(gradient)
            stressed.append([magnitude * part for part in parts])
            if 2 <= index < cells + 2:
                cell = index - 2
                points = points + [around(field, index, 3, block)]
                gradient = gradient + [[points[3][1 + j][1] - points[3][1 + j][0] for j in range(3)]]
                speed = [0.5 * points[j][0][:, :span] for j in range(3)]
                own_magnitude = magnitude[:, :span]
                strength[cell, out_rows, :] = own_magnitude
                for c in range(4):
                    middle, along, across, upward = points[c]
                    laplace = (
                        (along[0] + along[1]) + (across[0] + across[1]) + (upward[0] + upward[1])
                    )[:, :span] - 6.0 * middle[:, :span]
                    advection = (
                        speed[0] * gradient[c][0][:, :span]
                        + speed[1] * gradient[c][1][:, :span]
                        + speed[2] * gradient[c][2][:, :span]
                    )
                    molecular = gas_viscosity if c < 3 else gas_diffusivity
                    base_ref[c, cell, out_rows, :] = molecular * laplace - advection
                    eddy = own_magnitude * laplace
                    eddy_ref[c, cell, out_rows, :] = eddy if c < 3 else eddy * (1.0 / turbulent_prandtl)
        filtered = []
        for k, (i, j) in enumerate(PAIRS):
            pair = [stressed[x][k] + stressed[x + 1][k] for x in range(cells + 1)]
            filtered.append([binomial(pair[x] + pair[x + 1])[:, :span] for x in range(cells)])
        products = []
        for i, j in PAIRS:
            values = [
                field[x, i, place, :] * field[x, j, place, :] for x in range(1, cells + 3)
            ]
            pair = [values[x] + values[x + 1] for x in range(cells + 1)]
            products.append([binomial(pair[x] + pair[x + 1])[:, :span] for x in range(cells)])
        tile = carry
        first = block * 2 * cells
        for cell in range(cells):
            points = [around(coarse, cell + 1, c, block) for c in range(3)]
            gradient = [[(p[1 + j][1] - p[1 + j][0])[:, :span] for j in range(3)] for p in points]
            parts, magnitude = strain(gradient)
            quarter = 0.25 * magnitude
            speed = [0.25 * p[0][:, :span] for p in points]
            numerator = diagonal = off = 0.0
            for k, (i, j) in enumerate(PAIRS):
                model = filtered[k][cell] - quarter * parts[k]
                leonard = products[k][cell] - speed[i] * speed[j]
                numerator = numerator + leonard * model
                if i == j:
                    diagonal = diagonal + model * model
                else:
                    off = off + model * model
            denominator = diagonal + 0.5 * off
            total = jnp.sum(numerator, axis=1, keepdims=True) * (1.0 / 512.0)
            tile = jnp.where(column == first + cell, total, tile)
            total = jnp.sum(denominator, axis=1, keepdims=True) * (1.0 / 1024.0)
            tile = jnp.where(column == first + cells + cell, total, tile)
        return tile

    none = jnp.zeros((SUB, LANES), jnp.float32)
    sums_ref[0:SUB, :] = lax.fori_loop(0, rows // SUB, rate_block, none)
    tiles = span // LANES
    for cell in range(cells):
        planes = (
            strength[cell, 0:1, :],
            own_ref[0, cell, 0:1, :],
            own_ref[3, cell, 0:1, :],
        )
        for p, plane in enumerate(planes):
            for t in range(tiles):
                at = SUB + (p * cells + cell) * tiles + t
                sums_ref[at : at + 1, :] = plane[:, t * LANES : (t + 1) * LANES]


def lilly(total, cells, span_cells):
    mean_numerator = total / span_cells
    mean_denominator = shift_lanes(total, -cells) / span_cells
    return -mean_numerator / (2.0 * (mean_denominator + epsilon))


def merge_messages(mine_ref, theirs_ref, out_ref):
    held = mine_ref.shape[0]
    out_ref[0:SUB, :] = mine_ref[0:SUB, :] + theirs_ref[0:SUB, :]
    out_ref[SUB:held, :] = mine_ref[SUB:held, :]
    out_ref[held : 2 * held - SUB, :] = theirs_ref[SUB:held, :]


def finish_gas(span_cells, mine_ref, theirs_ref, base_ref, eddy_ref, out_ref):
    _, cells, rows, _ = base_ref.shape
    coefficient = lilly(mine_ref[0:SUB, :] + theirs_ref[0:SUB, :], cells, span_cells)
    for cell in range(cells):
        for block in range(rows // SUB):
            at = block * 2 * cells + cell
            factor = coefficient[:, at : at + 1]
            here = slice(SUB * block, SUB * (block + 1))
            for component in range(4):
                out_ref[component, cell, here, :] = (
                    base_ref[component, cell, here, :] + factor * eddy_ref[component, cell, here, :]
                )


def wall_fluxes(span_cells, devices, span, mine_ref, theirs_ref, wall_ref):
    cells = wall_ref.shape[0] // 2
    coefficient = lilly(mine_ref[0:SUB, :] + theirs_ref[0:SUB, :], cells, span_cells)
    tiles = span // LANES
    held = (mine_ref.shape[0] - SUB) // (devices // 2)
    for cell in range(cells):
        factor = coefficient[0:1, cell : cell + 1]
        for device in range(devices):
            ref = mine_ref if device < devices // 2 else theirs_ref
            start = SUB + device % (devices // 2) * held
            for t in range(tiles):
                strength, speed, heat = (
                    ref[at : at + 1, :]
                    for at in (start + (p * cells + cell) * tiles + t for p in range(3))
                )
                eddy = factor * strength
                place = pl.ds((device * tiles + t) * LANES, LANES)
                wall_ref[cell : cell + 1, place] = (gas_viscosity + eddy) * 2.0 * speed
                wall_ref[cells + cell : cells + cell + 1, place] = (
                    (gas_diffusivity + eddy / turbulent_prandtl) * 2.0 * heat
                )


def surface_flux(wall_ref, mask_ref, flux_ref):
    cells = mask_ref.shape[0]
    top = lax.axis_index("sa") == 0
    shear = mask_ref[...].astype(jnp.float32) * wall_ref[0:cells, :]
    flux_ref[0:cells, :] = jnp.where(top, shear, 0.0)
    flux_ref[cells:, :] = jnp.where(top, wall_ref[cells:, :], 0.0)


def finish(
    rate_ref,
    flux_ref,
    inside_ref,
    beside_mate_ref,
    beside_cross_ref,
    level_ref,
    gas_hbm,
    out_hbm,
    out_ref,
    gas_sem,
    sems,
):
    components, cells, depth, width = inside_ref.shape
    position = lax.axis_index("sa")
    even = lax.axis_index("gx") % 2 == 0
    level_id = lax.broadcasted_iota(jnp.int32, (SUB, width), 0)
    copies = [pltpu.make_async_copy(rate_ref, gas_hbm, gas_sem)]
    copies[0].start()
    for cell in range(cells):
        levels = level_ref[cell : cell + 1, :]
        for component in range(components):
            share = melt_viscosity if component == 0 else melt_diffusivity
            for block in range(depth // SUB):
                here = slice(SUB * block, SUB * (block + 1))
                rate = inside_ref[component, cell, here, :]
                if cell in (0, cells - 1):
                    from_mate = beside_mate_ref[component, here, :]
                    from_cross = beside_cross_ref[component, here, :]
                    outer = jnp.where(even == (cell == 0), from_cross, from_mate)
                    rate = rate + share * outer
                if block == 0:
                    flux = flux_ref[component * cells + cell : component * cells + cell + 1, :]
                    rate = rate + jnp.where(level_id == 0, flux, 0.0)
                if component == 0:
                    index = position * depth + SUB * block + level_id
                    rate = jnp.where(index >= levels, 0.0, rate)
                out_ref[component, cell, here, :] = rate
            copy = pltpu.make_async_copy(
                out_ref.at[component, cell], out_hbm.at[component, cell], sems.at[component, cell]
            )
            copy.start()
            copies = copies + [copy]
    for copy in copies:
        copy.wait()


def melt_inside(devices, melt_ref, mate_ref, cross_ref, mask_ref, level_ref, after_ref, part_ref, inside_ref, levels_ref):
    components, cells, depth, width = melt_ref.shape
    assert cells > 1
    pack_melt(0, melt_ref, part_ref)
    levels_ref[...] = level_ref[...]
    position = lax.axis_index("sa")
    even = position % 2 == 0
    top = position == 0
    level_id = lax.broadcasted_iota(jnp.int32, (SUB, width), 0)

    def row_of(ref, at):
        step = components * cells
        return jnp.concatenate(
            [ref[at + t * step : at + t * step + 1, :] for t in range(width // LANES)], axis=1
        )

    for cell in range(cells):
        mask = mask_ref[cell : cell + 1, :]
        for component in range(components):
            at = SUB + component * cells + cell
            from_mate, from_cross = row_of(mate_ref, at), row_of(cross_ref, at)
            first = melt_ref[component, cell, 0:1, :]
            ghost = jnp.where(mask == 1, first, -first) if component == 0 else first
            upper = jnp.where(top, ghost, jnp.where(even, from_cross, from_mate))
            final = melt_ref[component, cell, depth - 1 : depth, :]
            lower = jnp.where(position == devices - 1, final, jnp.where(even, from_mate, from_cross))
            for block in range(depth // SUB):
                here = slice(SUB * block, SUB * (block + 1))
                middle = melt_ref[component, cell, here, :]
                over = (
                    jnp.where(level_id == 0, upper, pltpu.roll(middle, 1, 0))
                    if block == 0
                    else melt_ref[component, cell, SUB * block - 1 : SUB * (block + 1) - 1, :]
                )
                under = (
                    jnp.where(level_id == SUB - 1, lower, pltpu.roll(middle, SUB - 1, 0))
                    if block == depth // SUB - 1
                    else melt_ref[component, cell, SUB * block + 1 : SUB * (block + 1) + 1, :]
                )
                laplace = (over + under) + (shift_lanes(middle, 1) + shift_lanes(middle, -1))
                for near in (cell - 1, cell + 1):
                    if 0 <= near < cells:
                        laplace = laplace + melt_ref[component, near, here, :]
                laplace = laplace - 6.0 * middle
                inside_ref[component, cell, here, :] = (
                    melt_viscosity if component == 0 else melt_diffusivity
                ) * laplace


def swap(source, axis, mask):
    return lax.ppermute(source, axis, [(i, i ^ mask) for i in range(lax.axis_size(axis))])


def swap_across(source, axis):
    count = lax.axis_size(axis)
    pairs = [(i, (i + 1) % count) for i in range(1, count, 2)]
    return lax.ppermute(source, axis, pairs + [(j, i) for i, j in pairs])


def swap_aside(source, first, aside):
    count, devices = lax.axis_size("gx"), lax.axis_size("sa")
    pairs = []
    for i in range(first, count, 2):
        j = (i + 1) % count
        for s in range(devices):
            t = s ^ 2 if aside else s
            pairs = pairs + [(i * devices + s, j * devices + t), (j * devices + s, i * devices + t)]
    return lax.ppermute(source, ("gx", "sa"), pairs)


def exchange(message, axis):
    count = lax.axis_size(axis)
    mask = 1
    while True:
        other = swap(message, axis, mask)
        mask = 2 * mask
        if mask == count:
            return message, other
        merged = array(2 * message.shape[0] - SUB, LANES)
        message = call(merge_messages, merged, [VMEM, VMEM])(message, other)


def fenced(part, *arrays):
    def no_part(*arrays):
        shapes = jax.eval_shape(part, *arrays)
        return jax.tree.map(lambda leaf: jnp.zeros(leaf.shape, leaf.dtype), shapes)

    return lax.cond(lax.axis_index("sa") < lax.axis_size("sa"), part, no_part, *arrays)


def call(kernel, outs, specs, scratch=(), flops=1, out_specs=None):
    return pl.pallas_call(
        kernel,
        out_shape=outs,
        in_specs=specs,
        out_specs=out_specs or jax.tree.map(lambda _: VMEM, outs),
        scratch_shapes=scratch,
        compiler_params=pltpu.CompilerParams(vmem_limit_bytes=24 * 1024 * 1024),
        cost_estimate=pl.CostEstimate(flops=flops, bytes_accessed=1, transcendentals=0),
    )


def array(*shape):
    return jax.ShapeDtypeStruct(shape, jnp.float32)


def on_device(gas, melt, surface_mask, melt_level):
    _, cells, rows, span = gas.shape
    components, _, depth, width = melt.shape
    devices = lax.axis_size("sa")
    assert devices & (devices - 1) == 0 and devices > 1
    span_cells = float(span * devices)
    even = lax.axis_index("sa") % 2 == 0
    gas_mate = swap(gas, "gx", 1)
    side = array(SUB + components * cells * width // LANES, LANES)
    mate, cross, gas_here = call(
        pack_sides,
        (side, side, array(*gas.shape)),
        [HBM, HBM],
        scratch=(
            pltpu.VMEM((2, components, cells, SUB, width), jnp.float32),
            pltpu.SemaphoreType.DMA((3,)),
        ),
    )(pltpu.with_memory_space_constraint(gas, pltpu.HBM), pltpu.with_memory_space_constraint(melt, pltpu.HBM))
    gas_cross = swap_across(gas_here, "gx")
    mate, cross = swap(mate, "sa", 1), swap_across(cross, "sa")
    late = lax.broadcasted_iota(jnp.int32, (SUB, LANES), 1) % EDGE >= EDGE // 2
    halo = jnp.where(late == even, cross[:SUB], mate[:SUB])
    aside = devices == 4
    passed = jnp.where(late == even, mate[:SUB], cross[:SUB]) if aside else halo
    halo_mate, halo_cross = swap_aside(passed, 0, aside), swap_aside(passed, 1, aside)
    part, whole = array(components, depth, width), array(components, cells, depth, width)
    levels = jax.ShapeDtypeStruct(melt_level.shape, jnp.int32)
    mate_part, inside, levels = call(
        functools.partial(melt_inside, devices), (part, whole, levels), [VMEM] * 5 + [ANY]
    )(melt, mate, cross, surface_mask, melt_level, halo_mate)
    cross_part = call(functools.partial(pack_melt, 1), part, [VMEM, ANY, ANY])(
        melt, gas_mate, mate_part
    )
    beside_mate = swap(mate_part, "gx", 1)
    beside_cross = swap_across(cross_part, "gx")

    def gas_part(*arrays):
        wide = span + LANES
        message_rows = SUB + 3 * cells * (span // LANES)
        base, eddy, message = call(
            germano,
            (array(4, cells, rows, span), array(4, cells, rows, span), array(message_rows, LANES)),
            [VMEM] * 6,
            scratch=(
                pltpu.VMEM((cells + 4, 4, rows + 2 * SUB, wide), jnp.float32),
                pltpu.VMEM((cells + 2, 3, rows + 2 * SUB, wide), jnp.float32),
                pltpu.VMEM((cells, rows, span), jnp.float32),
            ),
        )(*arrays)
        mine, theirs = exchange(message, "sa")
        rate = call(
            functools.partial(finish_gas, span_cells), array(4, cells, rows, span), [VMEM] * 4
        )(mine, theirs, base, eddy)
        wall = call(
            functools.partial(wall_fluxes, span_cells, devices, span),
            array(2 * cells, width),
            [VMEM, VMEM],
        )(mine, theirs)
        return rate, wall

    gas_rate, wall = fenced(
        gas_part, gas_here, gas_cross, gas_mate, halo, halo_mate, halo_cross
    )
    flux = call(surface_flux, array(2 * cells, width), [VMEM, VMEM], flops=4000000000)(
        wall, surface_mask
    )
    return call(
        finish,
        (array(4, cells, rows, span), whole),
        [VMEM] * 6,
        scratch=(
            pltpu.VMEM((components, cells, depth, width), jnp.float32),
            pltpu.SemaphoreType.DMA,
            pltpu.SemaphoreType.DMA((components, cells)),
        ),
        out_specs=(HBM, HBM),
    )(gas_rate, flux, inside, beside_mate, beside_cross, levels)


def solution(mesh):
    in_specs = (P(None, "gx", None, "sa"), P(None, "gx", "sa", None), P("gx", None), P("gx", None))
    out_specs = (P(None, "gx", None, "sa"), P(None, "gx", "sa", None))
    return jax.shard_map(
        on_device, mesh=mesh, in_specs=in_specs, out_specs=out_specs, check_vma=False
    )
```

```python
import functools

import jax
import jax.numpy as jnp
from jax import lax
from jax.experimental import pallas as pl
from jax.experimental.pallas import tpu as pltpu
from jax.sharding import PartitionSpec as P

gas_viscosity = 0.05
gas_diffusivity = 0.07
turbulent_prandtl = 0.85
melt_viscosity = 0.2
melt_diffusivity = 0.5
epsilon = 1e-06

LANES = 128
SUB = 8
EDGE = 4
PAIRS = ((0, 0), (1, 1), (2, 2), (0, 1), (0, 2), (1, 2))
VMEM = pl.BlockSpec(memory_space=pltpu.VMEM)
ANY = pl.BlockSpec(memory_space=pl.ANY)
HBM = pl.BlockSpec(memory_space=pltpu.HBM)


def shift_lanes(source, amount):
    extent = source.shape[-1]
    return pltpu.roll(source, amount % extent, source.ndim - 1)


def slot(row_block, cell, component, cells):
    return ((row_block * cells + cell) * 4 + component) * EDGE


def pack_sides(gas_hbm, melt_hbm, mate_ref, cross_ref, gas_ref, ends_ref, sems):
    _, cells, rows, span = gas_ref.shape
    components, _, depth, width = melt_hbm.shape
    copies = [pltpu.make_async_copy(gas_hbm, gas_ref, sems.at[0])]
    for end, start in enumerate((0, depth - SUB)):
        levels = melt_hbm.at[:, :, pl.ds(start, SUB), :]
        copies.append(pltpu.make_async_copy(levels, ends_ref.at[end], sems.at[end + 1]))
    for copy in copies:
        copy.start()
    copies[0].wait()
    lane = lax.broadcasted_iota(jnp.int32, (SUB, LANES), 1)
    tile = jnp.zeros((SUB, LANES), jnp.float32)
    for block in range(rows // SUB):
        for cell in range(cells):
            for component in range(4):
                at = slot(block, cell, component, cells)
                here = pl.ds(SUB * block, SUB)
                first = gas_ref[component, cell, here, 0:LANES]
                last = gas_ref[component, cell, here, span - LANES : span]
                tile = jnp.where((lane >= at) & (lane < at + 2), shift_lanes(first, at), tile)
                tile = jnp.where(
                    (lane >= at + 2) & (lane < at + 4), shift_lanes(last, at + 4), tile
                )
    mate_ref[0:SUB, :] = tile
    cross_ref[0:SUB, :] = tile
    even = lax.axis_index("sa") % 2 == 0
    for copy in copies[1:]:
        copy.wait()
    for component in range(components):
        for cell in range(cells):
            first = ends_ref[0, component, cell, 0:1, :]
            last = ends_ref[1, component, cell, SUB - 1 : SUB, :]
            mate = jnp.where(even, last, first)
            cross = jnp.where(even, first, last)
            for t in range(width // LANES):
                at = SUB + t * components * cells + component * cells + cell
                mate_ref[at : at + 1, :] = mate[:, t * LANES : (t + 1) * LANES]
                cross_ref[at : at + 1, :] = cross[:, t * LANES : (t + 1) * LANES]


def pack_melt(first, melt_ref, *refs):
    out_ref = refs[-1]
    last = melt_ref.shape[1] - 1
    lower = lax.axis_index("gx") % 2 == first

    @pl.when(lower)
    def _():
        out_ref[...] = melt_ref[:, last]

    @pl.when(jnp.logical_not(lower))
    def _():
        out_ref[...] = melt_ref[:, 0]


def binomial(source):
    return (shift_lanes(source, 1) + shift_lanes(source, -1)) + 2.0 * source


def germano(
    own_ref,
    cross_ref,
    mate_ref,
    halo_ref,
    halo_mate_ref,
    halo_cross_ref,
    base_ref,
    eddy_ref,
    sums_ref,
    field,
    coarse,
    strength,
):
    _, cells, rows, span = own_ref.shape
    wide = span + LANES
    lane = lax.broadcasted_iota(jnp.int32, (SUB, LANES), 1)
    even = lax.axis_index("gx") % 2 == 0
    halo = halo_ref[...]
    halo_left = jnp.where(even, halo_cross_ref[...], halo_mate_ref[...])
    halo_right = jnp.where(even, halo_mate_ref[...], halo_cross_ref[...])
    for index in range(cells + 4):
        if index < 2:
            columns, cell = halo_left, index + cells - 2
            sources = cross_ref, mate_ref
        elif index < cells + 2:
            columns, cell = halo, index - 2
            sources = own_ref, own_ref
        else:
            columns, cell = halo_right, index - cells - 2
            sources = mate_ref, cross_ref
        for component in range(4 if 1 <= index <= cells + 2 else 3):
            for block in range(rows // SUB):
                at = slot(block, cell, component, cells)
                place = pl.ds(SUB * (block + 1), SUB)
                here = slice(SUB * block, SUB * (block + 1))
                field[index, component, place, 0:span] = jnp.where(
                    even, sources[0][component, cell, here, :], sources[1][component, cell, here, :]
                )
                field[index, component, place, span:wide] = jnp.where(
                    lane < LANES // 2,
                    shift_lanes(columns, -at),
                    shift_lanes(columns, LANES - 4 - at),
                )
            field[index, component, SUB - 1 : SUB, :] = -field[index, component, SUB : SUB + 1, :]
            field[index, component, SUB + rows : SUB + rows + 1, :] = field[
                index, component, SUB + rows - 1 : SUB + rows, :
            ]

    def filter_block(block, carry):
        place = pl.ds(pl.multiple_of(SUB * (block + 1), SUB), SUB)
        for component in range(3):
            pair = [
                field[i, component, place, :] + field[i + 1, component, place, :]
                for i in range(cells + 3)
            ]
            for i in range(cells + 2):
                coarse[i, component, place, :] = binomial(pair[i] + pair[i + 1])
        return carry

    lax.fori_loop(0, rows // SUB, filter_block, 0, unroll=2)
    for i in range(cells + 2):
        for component in range(3):
            coarse[i, component, SUB - 1 : SUB, :] = -coarse[i, component, SUB : SUB + 1, :]
            coarse[i, component, SUB + rows : SUB + rows + 1, :] = coarse[
                i, component, SUB + rows - 1 : SUB + rows, :
            ]

    row = lax.broadcasted_iota(jnp.int32, (SUB, wide), 0)

    def around(ref, index, component, block):
        previous, place, following = (
            pl.ds(pl.multiple_of(SUB * (block + step), SUB), SUB) for step in range(3)
        )
        middle = ref[index, component, place, :]
        below = jnp.where(row == SUB - 1, ref[index, component, previous, :], middle)
        above = jnp.where(row == 0, ref[index, component, following, :], middle)
        return (
            middle,
            (ref[index - 1, component, place, :], ref[index + 1, component, place, :]),
            (shift_lanes(middle, 1), shift_lanes(middle, -1)),
            (pltpu.roll(below, 1, 0), pltpu.roll(above, SUB - 1, 0)),
        )

    def strain(gradient):
        parts = [
            gradient[i][i] if i == j else gradient[i][j] + gradient[j][i] for i, j in PAIRS
        ]
        diagonal = parts[0] * parts[0] + parts[1] * parts[1] + parts[2] * parts[2]
        off = parts[3] * parts[3] + parts[4] * parts[4] + parts[5] * parts[5]
        return parts, jnp.sqrt(0.5 * diagonal + 0.25 * off)

    column = lax.broadcasted_iota(jnp.int32, (SUB, LANES), 1)

    def rate_block(block, carry):
        out_rows = pl.ds(pl.multiple_of(SUB * block, SUB), SUB)
        place = pl.ds(pl.multiple_of(SUB * (block + 1), SUB), SUB)
        stressed = []
        for index in range(1, cells + 3):
            points = [around(field, index, c, block) for c in range(3)]
            gradient = [[p[1 + j][1] - p[1 + j][0] for j in range(3)] for p in points]
            parts, magnitude = strain(gradient)
            stressed.append([magnitude * part for part in parts])
            if 2 <= index < cells + 2:
                cell = index - 2
                points = points + [around(field, index, 3, block)]
                gradient = gradient + [[points[3][1 + j][1] - points[3][1 + j][0] for j in range(3)]]
                speed = [0.5 * points[j][0][:, :span] for j in range(3)]
                own_magnitude = magnitude[:, :span]
                strength[cell, out_rows, :] = own_magnitude
                for c in range(4):
                    middle, along, across, upward = points[c]
                    laplace = (
                        (along[0] + along[1]) + (across[0] + across[1]) + (upward[0] + upward[1])
                    )[:, :span] - 6.0 * middle[:, :span]
                    advection = (
                        speed[0] * gradient[c][0][:, :span]
                        + speed[1] * gradient[c][1][:, :span]
                        + speed[2] * gradient[c][2][:, :span]
                    )
                    molecular = gas_viscosity if c < 3 else gas_diffusivity
                    base_ref[c, cell, out_rows, :] = molecular * laplace - advection
                    eddy = own_magnitude * laplace
                    eddy_ref[c, cell, out_rows, :] = eddy if c < 3 else eddy * (1.0 / turbulent_prandtl)
        filtered = []
        for k, (i, j) in enumerate(PAIRS):
            pair = [stressed[x][k] + stressed[x + 1][k] for x in range(cells + 1)]
            filtered.append([binomial(pair[x] + pair[x + 1])[:, :span] for x in range(cells)])
        products = []
        for i, j in PAIRS:
            values = [
                field[x, i, place, :] * field[x, j, place, :] for x in range(1, cells + 3)
            ]
            pair = [values[x] + values[x + 1] for x in range(cells + 1)]
            products.append([binomial(pair[x] + pair[x + 1])[:, :span] for x in range(cells)])
        tile = carry
        first = block * 2 * cells
        for cell in range(cells):
            points = [around(coarse, cell + 1, c, block) for c in range(3)]
            gradient = [[(p[1 + j][1] - p[1 + j][0])[:, :span] for j in range(3)] for p in points]
            parts, magnitude = strain(gradient)
            quarter = 0.25 * magnitude
            speed = [0.25 * p[0][:, :span] for p in points]
            numerator = diagonal = off = 0.0
            for k, (i, j) in enumerate(PAIRS):
                model = filtered[k][cell] - quarter * parts[k]
                leonard = products[k][cell] - speed[i] * speed[j]
                numerator = numerator + leonard * model
                if i == j:
                    diagonal = diagonal + model * model
                else:
                    off = off + model * model
            denominator = diagonal + 0.5 * off
            total = jnp.sum(numerator, axis=1, keepdims=True) * (1.0 / 512.0)
            tile = jnp.where(column == first + cell, total, tile)
            total = jnp.sum(denominator, axis=1, keepdims=True) * (1.0 / 1024.0)
            tile = jnp.where(column == first + cells + cell, total, tile)
        return tile

    none = jnp.zeros((SUB, LANES), jnp.float32)
    sums_ref[0:SUB, :] = lax.fori_loop(0, rows // SUB, rate_block, none)
    tiles = span // LANES
    for cell in range(cells):
        planes = (
            strength[cell, 0:1, :],
            own_ref[0, cell, 0:1, :],
            own_ref[3, cell, 0:1, :],
        )
        for p, plane in enumerate(planes):
            for t in range(tiles):
                at = SUB + (p * cells + cell) * tiles + t
                sums_ref[at : at + 1, :] = plane[:, t * LANES : (t + 1) * LANES]


def lilly(total, cells, span_cells):
    mean_numerator = total / span_cells
    mean_denominator = shift_lanes(total, -cells) / span_cells
    return -mean_numerator / (2.0 * (mean_denominator + epsilon))


def merge_messages(mine_ref, theirs_ref, out_ref):
    held = mine_ref.shape[0]
    out_ref[0:SUB, :] = mine_ref[0:SUB, :] + theirs_ref[0:SUB, :]
    out_ref[SUB:held, :] = mine_ref[SUB:held, :]
    out_ref[held : 2 * held - SUB, :] = theirs_ref[SUB:held, :]


def finish_gas(span_cells, mine_ref, theirs_ref, base_ref, eddy_ref, out_ref):
    _, cells, rows, _ = base_ref.shape
    coefficient = lilly(mine_ref[0:SUB, :] + theirs_ref[0:SUB, :], cells, span_cells)
    for cell in range(cells):
        for block in range(rows // SUB):
            at = block * 2 * cells + cell
            factor = coefficient[:, at : at + 1]
            here = slice(SUB * block, SUB * (block + 1))
            for component in range(4):
                out_ref[component, cell, here, :] = (
                    base_ref[component, cell, here, :] + factor * eddy_ref[component, cell, here, :]
                )


def wall_fluxes(span_cells, devices, span, mine_ref, theirs_ref, wall_ref):
    cells = wall_ref.shape[0] // 2
    coefficient = lilly(mine_ref[0:SUB, :] + theirs_ref[0:SUB, :], cells, span_cells)
    tiles = span // LANES
    held = (mine_ref.shape[0] - SUB) // (devices // 2)
    for cell in range(cells):
        factor = coefficient[0:1, cell : cell + 1]
        for device in range(devices):
            ref = mine_ref if device < devices // 2 else theirs_ref
            start = SUB + device % (devices // 2) * held
            for t in range(tiles):
                strength, speed, heat = (
                    ref[at : at + 1, :]
                    for at in (start + (p * cells + cell) * tiles + t for p in range(3))
                )
                eddy = factor * strength
                place = pl.ds((device * tiles + t) * LANES, LANES)
                wall_ref[cell : cell + 1, place] = (gas_viscosity + eddy) * 2.0 * speed
                wall_ref[cells + cell : cells + cell + 1, place] = (
                    (gas_diffusivity + eddy / turbulent_prandtl) * 2.0 * heat
                )


def surface_flux(wall_ref, mask_ref, flux_ref):
    cells = mask_ref.shape[0]
    top = lax.axis_index("sa") == 0
    shear = mask_ref[...].astype(jnp.float32) * wall_ref[0:cells, :]
    flux_ref[0:cells, :] = jnp.where(top, shear, 0.0)
    flux_ref[cells:, :] = jnp.where(top, wall_ref[cells:, :], 0.0)


def finish(
    rate_ref,
    flux_ref,
    inside_ref,
    beside_mate_ref,
    beside_cross_ref,
    level_ref,
    gas_hbm,
    out_hbm,
    out_ref,
    gas_sem,
    sems,
):
    components, cells, depth, width = inside_ref.shape
    position = lax.axis_index("sa")
    even = lax.axis_index("gx") % 2 == 0
    level_id = lax.broadcasted_iota(jnp.int32, (SUB, width), 0)
    copies = [pltpu.make_async_copy(rate_ref, gas_hbm, gas_sem)]
    copies[0].start()
    for cell in range(cells):
        levels = level_ref[cell : cell + 1, :]
        for component in range(components):
            share = melt_viscosity if component == 0 else melt_diffusivity
            for block in range(depth // SUB):
                here = slice(SUB * block, SUB * (block + 1))
                rate = inside_ref[component, cell, here, :]
                if cell in (0, cells - 1):
                    from_mate = beside_mate_ref[component, here, :]
                    from_cross = beside_cross_ref[component, here, :]
                    outer = jnp.where(even == (cell == 0), from_cross, from_mate)
                    rate = rate + share * outer
                if block == 0:
                    flux = flux_ref[component * cells + cell : component * cells + cell + 1, :]
                    rate = rate + jnp.where(level_id == 0, flux, 0.0)
                if component == 0:
                    index = position * depth + SUB * block + level_id
                    rate = jnp.where(index >= levels, 0.0, rate)
                out_ref[component, cell, here, :] = rate
            copy = pltpu.make_async_copy(
                out_ref.at[component, cell], out_hbm.at[component, cell], sems.at[component, cell]
            )
            copy.start()
            copies = copies + [copy]
    for copy in copies:
        copy.wait()


def melt_inside(devices, melt_ref, mate_ref, cross_ref, mask_ref, level_ref, after_ref, part_ref, inside_ref, levels_ref):
    components, cells, depth, width = melt_ref.shape
    assert cells > 1
    pack_melt(0, melt_ref, part_ref)
    levels_ref[...] = level_ref[...]
    position = lax.axis_index("sa")
    even = position % 2 == 0
    top = position == 0
    level_id = lax.broadcasted_iota(jnp.int32, (SUB, width), 0)

    def row_of(ref, at):
        step = components * cells
        return jnp.concatenate(
            [ref[at + t * step : at + t * step + 1, :] for t in range(width // LANES)], axis=1
        )

    for cell in range(cells):
        mask = mask_ref[cell : cell + 1, :]
        for component in range(components):
            at = SUB + component * cells + cell
            from_mate, from_cross = row_of(mate_ref, at), row_of(cross_ref, at)
            first = melt_ref[component, cell, 0:1, :]
            ghost = jnp.where(mask == 1, first, -first) if component == 0 else first
            upper = jnp.where(top, ghost, jnp.where(even, from_cross, from_mate))
            final = melt_ref[component, cell, depth - 1 : depth, :]
            lower = jnp.where(position == devices - 1, final, jnp.where(even, from_mate, from_cross))
            for block in range(depth // SUB):
                here = slice(SUB * block, SUB * (block + 1))
                middle = melt_ref[component, cell, here, :]
                over = (
                    jnp.where(level_id == 0, upper, pltpu.roll(middle, 1, 0))
                    if block == 0
                    else melt_ref[component, cell, SUB * block - 1 : SUB * (block + 1) - 1, :]
                )
                under = (
                    jnp.where(level_id == SUB - 1, lower, pltpu.roll(middle, SUB - 1, 0))
                    if block == depth // SUB - 1
                    else melt_ref[component, cell, SUB * block + 1 : SUB * (block + 1) + 1, :]
                )
                laplace = (over + under) + (shift_lanes(middle, 1) + shift_lanes(middle, -1))
                for near in (cell - 1, cell + 1):
                    if 0 <= near < cells:
                        laplace = laplace + melt_ref[component, near, here, :]
                laplace = laplace - 6.0 * middle
                inside_ref[component, cell, here, :] = (
                    melt_viscosity if component == 0 else melt_diffusivity
                ) * laplace


def swap(source, axis, mask):
    return lax.ppermute(source, axis, [(i, i ^ mask) for i in range(lax.axis_size(axis))])


def swap_across(source, axis):
    count = lax.axis_size(axis)
    pairs = [(i, (i + 1) % count) for i in range(1, count, 2)]
    return lax.ppermute(source, axis, pairs + [(j, i) for i, j in pairs])


def swap_aside(source, first, aside):
    count, devices = lax.axis_size("gx"), lax.axis_size("sa")
    pairs = []
    for i in range(first, count, 2):
        j = (i + 1) % count
        for s in range(devices):
            t = s ^ 2 if aside else s
            pairs = pairs + [(i * devices + s, j * devices + t), (j * devices + s, i * devices + t)]
    return lax.ppermute(source, ("gx", "sa"), pairs)


def exchange(message, axis):
    count = lax.axis_size(axis)
    mask = 1
    while True:
        other = swap(message, axis, mask)
        mask = 2 * mask
        if mask == count:
            return message, other
        merged = array(2 * message.shape[0] - SUB, LANES)
        message = call(merge_messages, merged, [VMEM, VMEM])(message, other)


def fenced(part, *arrays):
    def no_part(*arrays):
        shapes = jax.eval_shape(part, *arrays)
        return jax.tree.map(lambda leaf: jnp.zeros(leaf.shape, leaf.dtype), shapes)

    return lax.cond(lax.axis_index("sa") < lax.axis_size("sa"), part, no_part, *arrays)


def call(kernel, outs, specs, scratch=(), flops=1, out_specs=None):
    return pl.pallas_call(
        kernel,
        out_shape=outs,
        in_specs=specs,
        out_specs=out_specs or jax.tree.map(lambda _: VMEM, outs),
        scratch_shapes=scratch,
        compiler_params=pltpu.CompilerParams(vmem_limit_bytes=24 * 1024 * 1024),
        cost_estimate=pl.CostEstimate(flops=flops, bytes_accessed=1, transcendentals=0),
    )


def array(*shape):
    return jax.ShapeDtypeStruct(shape, jnp.float32)


def on_device(gas, melt, surface_mask, melt_level):
    _, cells, rows, span = gas.shape
    components, _, depth, width = melt.shape
    devices = lax.axis_size("sa")
    assert devices & (devices - 1) == 0 and devices > 1
    span_cells = float(span * devices)
    even = lax.axis_index("sa") % 2 == 0
    gas_mate = swap(gas, "gx", 1)
    side = array(SUB + components * cells * width // LANES, LANES)
    mate, cross, gas_here = call(
        pack_sides,
        (side, side, array(*gas.shape)),
        [HBM, HBM],
        scratch=(
            pltpu.VMEM((2, components, cells, SUB, width), jnp.float32),
            pltpu.SemaphoreType.DMA((3,)),
        ),
    )(pltpu.with_memory_space_constraint(gas, pltpu.HBM), pltpu.with_memory_space_constraint(melt, pltpu.HBM))
    gas_cross = swap_across(gas_here, "gx")
    mate, cross = swap(mate, "sa", 1), swap_across(cross, "sa")
    late = lax.broadcasted_iota(jnp.int32, (SUB, LANES), 1) % EDGE >= EDGE // 2
    halo = jnp.where(late == even, cross[:SUB], mate[:SUB])
    aside = devices == 4
    passed = jnp.where(late == even, mate[:SUB], cross[:SUB]) if aside else halo
    halo_mate, halo_cross = swap_aside(passed, 0, aside), swap_aside(passed, 1, aside)
    part, whole = array(components, depth, width), array(components, cells, depth, width)
    levels = jax.ShapeDtypeStruct(melt_level.shape, jnp.int32)
    mate_part, inside, levels = call(
        functools.partial(melt_inside, devices), (part, whole, levels), [VMEM] * 5 + [ANY]
    )(melt, mate, cross, surface_mask, melt_level, halo_mate)
    cross_part = call(functools.partial(pack_melt, 1), part, [VMEM, ANY, ANY])(
        melt, gas_mate, mate_part
    )
    beside_mate = swap(mate_part, "gx", 1)
    beside_cross = swap_across(cross_part, "gx")

    def gas_part(*arrays):
        wide = span + LANES
        message_rows = SUB + 3 * cells * (span // LANES)
        base, eddy, message = call(
            germano,
            (array(4, cells, rows, span), array(4, cells, rows, span), array(message_rows, LANES)),
            [VMEM] * 6,
            scratch=(
                pltpu.VMEM((cells + 4, 4, rows + 2 * SUB, wide), jnp.float32),
                pltpu.VMEM((cells + 2, 3, rows + 2 * SUB, wide), jnp.float32),
                pltpu.VMEM((cells, rows, span), jnp.float32),
            ),
        )(*arrays)
        mine, theirs = exchange(message, "sa")
        rate = call(
            functools.partial(finish_gas, span_cells), array(4, cells, rows, span), [VMEM] * 4
        )(mine, theirs, base, eddy)
        wall = call(
            functools.partial(wall_fluxes, span_cells, devices, span),
            array(2 * cells, width),
            [VMEM, VMEM],
        )(mine, theirs)
        return rate, wall

    gas_rate, wall = fenced(
        gas_part, gas_here, gas_cross, gas_mate, halo, halo_mate, halo_cross
    )
    flux = call(surface_flux, array(2 * cells, width), [VMEM, VMEM], flops=4000000000)(
        wall, surface_mask
    )
    return call(
        finish,
        (array(4, cells, rows, span), whole),
        [VMEM] * 6,
        scratch=(
            pltpu.VMEM((components, cells, depth, width), jnp.float32),
            pltpu.SemaphoreType.DMA,
            pltpu.SemaphoreType.DMA((components, cells)),
        ),
        out_specs=(HBM, HBM),
    )(gas_rate, flux, inside, beside_mate, beside_cross, levels)


def solution(mesh):
    in_specs = (P(None, "gx", None, "sa"), P(None, "gx", "sa", None), P("gx", None), P("gx", None))
    out_specs = (P(None, "gx", None, "sa"), P(None, "gx", "sa", None))
    return jax.shard_map(
        on_device, mesh=mesh, in_specs=in_specs, out_specs=out_specs, check_vma=False
    )
```

```python
import functools

import jax
import jax.numpy as jnp
from jax import lax
from jax.experimental import pallas as pl
from jax.experimental.pallas import tpu as pltpu
from jax.sharding import PartitionSpec as P

gas_viscosity = 0.05
gas_diffusivity = 0.07
turbulent_prandtl = 0.85
melt_viscosity = 0.2
melt_diffusivity = 0.5
epsilon = 1e-06

LANES = 128
SUB = 8
EDGE = 4
PAIRS = ((0, 0), (1, 1), (2, 2), (0, 1), (0, 2), (1, 2))
VMEM = pl.BlockSpec(memory_space=pltpu.VMEM)
ANY = pl.BlockSpec(memory_space=pl.ANY)
HBM = pl.BlockSpec(memory_space=pltpu.HBM)


def shift_lanes(source, amount):
    extent = source.shape[-1]
    return pltpu.roll(source, amount % extent, source.ndim - 1)


def slot(row_block, cell, component, cells):
    return ((row_block * cells + cell) * 4 + component) * EDGE


def pack_sides(
    gas_hbm, melt_hbm, mate_ref, cross_ref, velocity_ref, heat_ref, ends_ref, sems
):
    cells, rows, span = heat_ref.shape
    components, _, depth, width = melt_hbm.shape
    copies = [pltpu.make_async_copy(gas_hbm.at[3], heat_ref, sems.at[2])]
    for component in range(3):
        place = pl.ds(component * cells, cells)
        copies.append(
            pltpu.make_async_copy(
                gas_hbm.at[component], velocity_ref.at[place], sems.at[3 + component]
            )
        )
    for end, start in enumerate((0, depth - SUB)):
        levels = melt_hbm.at[:, :, pl.ds(start, SUB), :]
        copies.append(pltpu.make_async_copy(levels, ends_ref.at[end], sems.at[end]))
    for copy in copies:
        copy.start()
    for copy in copies[:4]:
        copy.wait()
    lower = lax.axis_index("gx") % 2 == 1
    velocity_ref[3 * cells] = jnp.where(lower, heat_ref[cells - 1], heat_ref[0])
    lane = lax.broadcasted_iota(jnp.int32, (SUB, LANES), 1)
    tile = jnp.zeros((SUB, LANES), jnp.float32)
    for block in range(rows // SUB):
        for cell in range(cells):
            for component in range(4):
                at = slot(block, cell, component, cells)
                here = pl.ds(SUB * block, SUB)
                source = velocity_ref.at[component * cells + cell] if component < 3 else heat_ref.at[cell]
                first = source[here, 0:LANES]
                last = source[here, span - LANES : span]
                tile = jnp.where((lane >= at) & (lane < at + 2), shift_lanes(first, at), tile)
                tile = jnp.where(
                    (lane >= at + 2) & (lane < at + 4), shift_lanes(last, at + 4), tile
                )
    mate_ref[0:SUB, :] = tile
    cross_ref[0:SUB, :] = tile
    even = lax.axis_index("sa") % 2 == 0
    for copy in copies[4:]:
        copy.wait()
    for component in range(components):
        for cell in range(cells):
            first = ends_ref[0, component, cell, 0:1, :]
            last = ends_ref[1, component, cell, SUB - 1 : SUB, :]
            mate = jnp.where(even, last, first)
            cross = jnp.where(even, first, last)
            for t in range(width // LANES):
                at = SUB + t * components * cells + component * cells + cell
                mate_ref[at : at + 1, :] = mate[:, t * LANES : (t + 1) * LANES]
                cross_ref[at : at + 1, :] = cross[:, t * LANES : (t + 1) * LANES]


def pack_melt(first, melt_ref, *refs):
    out_ref = refs[-1]
    components, cells, depth, _ = melt_ref.shape
    lower = lax.axis_index("gx") % 2 == first

    def put(cell):
        for component in range(components):
            out_ref[component * depth : (component + 1) * depth, :] = melt_ref[component, cell]

    @pl.when(lower)
    def _():
        put(cells - 1)

    @pl.when(jnp.logical_not(lower))
    def _():
        put(0)


def binomial(source):
    return (shift_lanes(source, 1) + shift_lanes(source, -1)) + 2.0 * source


def germano(
    own_ref,
    cross_ref,
    mate_ref,
    heat_ref,
    halo_ref,
    halo_mate_ref,
    halo_cross_ref,
    base_ref,
    eddy_ref,
    strength,
    sums_ref,
    field,
    coarse,
):
    cells, rows, span = heat_ref.shape
    wide = span + LANES
    lane = lax.broadcasted_iota(jnp.int32, (SUB, LANES), 1)
    even = lax.axis_index("gx") % 2 == 0
    halo = halo_ref[...]
    halo_left = jnp.where(even, halo_cross_ref[...], halo_mate_ref[...])
    halo_right = jnp.where(even, halo_mate_ref[...], halo_cross_ref[...])
    for index in range(cells + 4):
        if index < 2:
            columns, cell = halo_left, index + cells - 2
            sources = cross_ref, mate_ref
        elif index < cells + 2:
            columns, cell = halo, index - 2
            sources = own_ref, own_ref
        else:
            columns, cell = halo_right, index - cells - 2
            sources = mate_ref, cross_ref
        for component in range(3):
            for block in range(rows // SUB):
                at = slot(block, cell, component, cells)
                place = pl.ds(SUB * (block + 1), SUB)
                here = slice(SUB * block, SUB * (block + 1))
                parts = [
                    ref[component, cell, here, :]
                    if ref is mate_ref
                    else ref[component * cells + cell, here, :]
                    for ref in sources
                ]
                field[index, component, place, 0:span] = jnp.where(even, parts[0], parts[1])
                field[index, component, place, span:wide] = jnp.where(
                    lane < LANES // 2,
                    shift_lanes(columns, -at),
                    shift_lanes(columns, LANES - 4 - at),
                )
            field[index, component, SUB - 1 : SUB, :] = -field[index, component, SUB : SUB + 1, :]
            field[index, component, SUB + rows : SUB + rows + 1, :] = field[
                index, component, SUB + rows - 1 : SUB + rows, :
            ]

    def filter_block(block, carry):
        place = pl.ds(pl.multiple_of(SUB * (block + 1), SUB), SUB)
        for component in range(3):
            pair = [
                field[i, component, place, :] + field[i + 1, component, place, :]
                for i in range(cells + 3)
            ]
            for i in range(cells + 2):
                coarse[i, component, place, :] = binomial(pair[i] + pair[i + 1])
        return carry

    lax.fori_loop(0, rows // SUB, filter_block, 0, unroll=2)
    for i in range(cells + 2):
        for component in range(3):
            coarse[i, component, SUB - 1 : SUB, :] = -coarse[i, component, SUB : SUB + 1, :]
            coarse[i, component, SUB + rows : SUB + rows + 1, :] = coarse[
                i, component, SUB + rows - 1 : SUB + rows, :
            ]

    row = lax.broadcasted_iota(jnp.int32, (SUB, wide), 0)

    def around(ref, index, component, block):
        previous, place, following = (
            pl.ds(pl.multiple_of(SUB * (block + step), SUB), SUB) for step in range(3)
        )
        middle = ref[index, component, place, :]
        below = jnp.where(row == SUB - 1, ref[index, component, previous, :], middle)
        above = jnp.where(row == 0, ref[index, component, following, :], middle)
        return (
            middle,
            (ref[index - 1, component, place, :], ref[index + 1, component, place, :]),
            (shift_lanes(middle, 1), shift_lanes(middle, -1)),
            (pltpu.roll(below, 1, 0), pltpu.roll(above, SUB - 1, 0)),
        )

    def strain(gradient):
        parts = [
            gradient[i][i] if i == j else gradient[i][j] + gradient[j][i] for i, j in PAIRS
        ]
        diagonal = parts[0] * parts[0] + parts[1] * parts[1] + parts[2] * parts[2]
        off = parts[3] * parts[3] + parts[4] * parts[4] + parts[5] * parts[5]
        return parts, jnp.sqrt(0.5 * diagonal + 0.25 * off)

    column = lax.broadcasted_iota(jnp.int32, (SUB, LANES), 1)

    def rate_block(block, carry):
        out_rows = pl.ds(pl.multiple_of(SUB * block, SUB), SUB)
        place = pl.ds(pl.multiple_of(SUB * (block + 1), SUB), SUB)
        stressed = []
        for index in range(1, cells + 3):
            points = [around(field, index, c, block) for c in range(3)]
            gradient = [[p[1 + j][1] - p[1 + j][0] for j in range(3)] for p in points]
            parts, magnitude = strain(gradient)
            stressed.append([magnitude * part for part in parts])
            if 2 <= index < cells + 2:
                cell = index - 2
                speed = [0.5 * points[j][0][:, :span] for j in range(3)]
                own_magnitude = magnitude[:, :span]
                strength[cell, out_rows, :] = own_magnitude
                for c in range(3):
                    middle, along, across, upward = points[c]
                    laplace = (
                        (along[0] + along[1]) + (across[0] + across[1]) + (upward[0] + upward[1])
                    )[:, :span] - 6.0 * middle[:, :span]
                    advection = (
                        speed[0] * gradient[c][0][:, :span]
                        + speed[1] * gradient[c][1][:, :span]
                        + speed[2] * gradient[c][2][:, :span]
                    )
                    base_ref[c, cell, out_rows, :] = gas_viscosity * laplace - advection
                    eddy_ref[c, cell, out_rows, :] = own_magnitude * laplace
        filtered = []
        for k, (i, j) in enumerate(PAIRS):
            pair = [stressed[x][k] + stressed[x + 1][k] for x in range(cells + 1)]
            filtered.append([binomial(pair[x] + pair[x + 1])[:, :span] for x in range(cells)])
        products = []
        for i, j in PAIRS:
            values = [
                field[x, i, place, :] * field[x, j, place, :] for x in range(1, cells + 3)
            ]
            pair = [values[x] + values[x + 1] for x in range(cells + 1)]
            products.append([binomial(pair[x] + pair[x + 1])[:, :span] for x in range(cells)])
        tile = carry
        first = block * 2 * cells
        for cell in range(cells):
            points = [around(coarse, cell + 1, c, block) for c in range(3)]
            gradient = [[(p[1 + j][1] - p[1 + j][0])[:, :span] for j in range(3)] for p in points]
            parts, magnitude = strain(gradient)
            quarter = 0.25 * magnitude
            speed = [0.25 * p[0][:, :span] for p in points]
            numerator = diagonal = off = 0.0
            for k, (i, j) in enumerate(PAIRS):
                model = filtered[k][cell] - quarter * parts[k]
                leonard = products[k][cell] - speed[i] * speed[j]
                numerator = numerator + leonard * model
                if i == j:
                    diagonal = diagonal + model * model
                else:
                    off = off + model * model
            denominator = diagonal + 0.5 * off
            total = jnp.sum(numerator, axis=1, keepdims=True) * (1.0 / 512.0)
            tile = jnp.where(column == first + cell, total, tile)
            total = jnp.sum(denominator, axis=1, keepdims=True) * (1.0 / 1024.0)
            tile = jnp.where(column == first + cells + cell, total, tile)
        return tile

    none = jnp.zeros((SUB, LANES), jnp.float32)
    sums_ref[0:SUB, :] = lax.fori_loop(0, rows // SUB, rate_block, none)
    tiles = span // LANES
    for cell in range(cells):
        planes = (
            strength[cell, 0:1, :],
            own_ref[cell, 0:1, :],
            heat_ref[cell, 0:1, :],
        )
        for p, plane in enumerate(planes):
            for t in range(tiles):
                at = SUB + (p * cells + cell) * tiles + t
                sums_ref[at : at + 1, :] = plane[:, t * LANES : (t + 1) * LANES]


def lilly(total, cells, span_cells):
    mean_numerator = total / span_cells
    mean_denominator = shift_lanes(total, -cells) / span_cells
    return -mean_numerator / (2.0 * (mean_denominator + epsilon))


def merge_messages(mine_ref, theirs_ref, out_ref):
    held = mine_ref.shape[0]
    out_ref[0:SUB, :] = mine_ref[0:SUB, :] + theirs_ref[0:SUB, :]
    out_ref[SUB:held, :] = mine_ref[SUB:held, :]
    out_ref[held : 2 * held - SUB, :] = theirs_ref[SUB:held, :]


def finish_gas(
    span_cells,
    mine_ref,
    theirs_ref,
    base_ref,
    eddy_ref,
    strength_ref,
    own_ref,
    heat_ref,
    halo_ref,
    rate_ref,
    inside_ref,
    share_ref,
):
    _, cells, rows, span = base_ref.shape
    coefficient = lilly(mine_ref[0:SUB, :] + theirs_ref[0:SUB, :], cells, span_cells)
    row = lax.broadcasted_iota(jnp.int32, (SUB, span), 0)
    lane = lax.broadcasted_iota(jnp.int32, (SUB, span), 1)
    for cell in range(cells):
        for block in range(rows // SUB):
            at = block * 2 * cells + cell
            factor = coefficient[:, at : at + 1]
            here = slice(SUB * block, SUB * (block + 1))
            for component in range(3):
                rate_ref[component, cell, here, :] = (
                    base_ref[component, cell, here, :] + factor * eddy_ref[component, cell, here, :]
                )
            middle = heat_ref[cell, here, :]
            at = slot(block, cell, 3, cells)
            behind = jnp.where(lane == 0, halo_ref[:, at + 3 : at + 4], shift_lanes(middle, 1))
            ahead = jnp.where(lane == span - 1, halo_ref[:, at : at + 1], shift_lanes(middle, -1))
            below = (
                jnp.where(row == 0, -middle, pltpu.roll(middle, 1, 0))
                if block == 0
                else heat_ref[cell, SUB * block - 1 : SUB * (block + 1) - 1, :]
            )
            above = (
                jnp.where(row == SUB - 1, middle, pltpu.roll(middle, SUB - 1, 0))
                if block == rows // SUB - 1
                else heat_ref[cell, SUB * block + 1 : SUB * (block + 1) + 1, :]
            )
            speed = [0.5 * own_ref[j * cells + cell, here, :] for j in range(3)]
            diffusivity = gas_diffusivity + factor * strength_ref[cell, here, :] * (
                1.0 / turbulent_prandtl
            )
            laplace = (behind + ahead) + (below + above) - 6.0 * middle
            advection = speed[1] * (ahead - behind) + speed[2] * (above - below)
            for near, sign in ((cell - 1, -1.0), (cell + 1, 1.0)):
                if 0 <= near < cells:
                    value = heat_ref[near, here, :]
                    laplace = laplace + value
                    advection = advection + sign * speed[0] * value
                else:
                    share_ref[0 if near < 0 else 1, here, :] = diffusivity - sign * speed[0]
            inside_ref[cell, here, :] = diffusivity * laplace - advection


def wall_fluxes(span_cells, devices, span, mine_ref, theirs_ref, wall_ref):
    cells = wall_ref.shape[0] // 2
    coefficient = lilly(mine_ref[0:SUB, :] + theirs_ref[0:SUB, :], cells, span_cells)
    tiles = span // LANES
    held = (mine_ref.shape[0] - SUB) // (devices // 2)
    for cell in range(cells):
        factor = coefficient[0:1, cell : cell + 1]
        for device in range(devices):
            ref = mine_ref if device < devices // 2 else theirs_ref
            start = SUB + device % (devices // 2) * held
            for t in range(tiles):
                strength, speed, heat = (
                    ref[at : at + 1, :]
                    for at in (start + (p * cells + cell) * tiles + t for p in range(3))
                )
                eddy = factor * strength
                place = pl.ds((device * tiles + t) * LANES, LANES)
                wall_ref[cell : cell + 1, place] = (gas_viscosity + eddy) * 2.0 * speed
                wall_ref[cells + cell : cells + cell + 1, place] = (
                    (gas_diffusivity + eddy / turbulent_prandtl) * 2.0 * heat
                )


def surface_flux(wall_ref, mask_ref, flux_ref):
    cells = mask_ref.shape[0]
    top = lax.axis_index("sa") == 0
    shear = mask_ref[...].astype(jnp.float32) * wall_ref[0:cells, :]
    flux_ref[0:cells, :] = jnp.where(top, shear, 0.0)
    flux_ref[cells:, :] = jnp.where(top, wall_ref[cells:, :], 0.0)


def finish(
    flux_ref,
    inside_ref,
    beside_mate_ref,
    beside_cross_ref,
    level_ref,
    rate_ref,
    heat_ref,
    share_ref,
    gas_mate_ref,
    gas_cross_ref,
    gas_hbm,
    melt_hbm,
    heat_out,
    melt_out,
    sems,
):
    components, cells, depth, width = inside_ref.shape
    _, rows, span = heat_ref.shape
    position = lax.axis_index("sa")
    even = lax.axis_index("gx") % 2 == 0
    level_id = lax.broadcasted_iota(jnp.int32, (SUB, width), 0)
    copies = [pltpu.make_async_copy(rate_ref, gas_hbm.at[pl.ds(0, 3)], sems.at[0])]
    copies[0].start()

    def beside(cell, here):
        from_mate = beside_mate_ref[here, :]
        return jnp.where(even == (cell == 0), beside_cross_ref[here, :], from_mate)

    for cell in range(cells):
        for component in range(components):
            share = melt_viscosity if component == 0 else melt_diffusivity
            for block in range(depth // SUB):
                here = slice(SUB * block, SUB * (block + 1))
                rate = inside_ref[component, cell, here, :]
                if cell in (0, cells - 1):
                    start = component * depth + SUB * block
                    rate = rate + share * beside(cell, slice(start, start + SUB))
                if block == 0:
                    flux = flux_ref[component * cells + cell : component * cells + cell + 1, :]
                    rate = rate + jnp.where(level_id == 0, flux, 0.0)
                if component == 0:
                    index = position * depth + SUB * block + level_id
                    rate = jnp.where(index >= level_ref[cell : cell + 1, :], 0.0, rate)
                melt_out[component, cell, here, :] = rate
            copies.append(
                pltpu.make_async_copy(
                    melt_out.at[component, cell],
                    melt_hbm.at[component, cell],
                    sems.at[2 + component * cells + cell],
                )
            )
            copies[-1].start()
    for cell in range(cells):
        for block in range(rows // SUB):
            here = slice(SUB * block, SUB * (block + 1))
            rate = heat_ref[cell, here, :]
            if cell in (0, cells - 1):
                share = share_ref[0 if cell == 0 else 1, here, :]
                from_cross = gas_cross_ref[gas_cross_ref.shape[0] - 1, here, :]
                from_mate = gas_mate_ref[3, cells - 1 if cell == 0 else 0, here, :]
                rate = rate + share * jnp.where(even == (cell == 0), from_cross, from_mate)
            heat_out[cell, here, :] = rate
    copies.append(pltpu.make_async_copy(heat_out, gas_hbm.at[3], sems.at[1]))
    copies[-1].start()
    for copy in copies:
        copy.wait()


def melt_inside(
    devices,
    melt_ref,
    heat_ref,
    mate_ref,
    cross_ref,
    mask_ref,
    level_ref,
    after_ref,
    part_ref,
    inside_ref,
    levels_ref,
):
    components, cells, depth, width = melt_ref.shape
    assert cells > 1
    pack_melt(0, melt_ref, heat_ref, part_ref)
    levels_ref[...] = level_ref[...]
    position = lax.axis_index("sa")
    even = position % 2 == 0
    top = position == 0
    level_id = lax.broadcasted_iota(jnp.int32, (SUB, width), 0)

    def row_of(ref, at):
        step = components * cells
        return jnp.concatenate(
            [ref[at + t * step : at + t * step + 1, :] for t in range(width // LANES)], axis=1
        )

    for cell in range(cells):
        mask = mask_ref[cell : cell + 1, :]
        for component in range(components):
            at = SUB + component * cells + cell
            from_mate, from_cross = row_of(mate_ref, at), row_of(cross_ref, at)
            first = melt_ref[component, cell, 0:1, :]
            ghost = jnp.where(mask == 1, first, -first) if component == 0 else first
            upper = jnp.where(top, ghost, jnp.where(even, from_cross, from_mate))
            final = melt_ref[component, cell, depth - 1 : depth, :]
            lower = jnp.where(position == devices - 1, final, jnp.where(even, from_mate, from_cross))
            for block in range(depth // SUB):
                here = slice(SUB * block, SUB * (block + 1))
                middle = melt_ref[component, cell, here, :]
                over = (
                    jnp.where(level_id == 0, upper, pltpu.roll(middle, 1, 0))
                    if block == 0
                    else melt_ref[component, cell, SUB * block - 1 : SUB * (block + 1) - 1, :]
                )
                under = (
                    jnp.where(level_id == SUB - 1, lower, pltpu.roll(middle, SUB - 1, 0))
                    if block == depth // SUB - 1
                    else melt_ref[component, cell, SUB * block + 1 : SUB * (block + 1) + 1, :]
                )
                laplace = (over + under) + (shift_lanes(middle, 1) + shift_lanes(middle, -1))
                for near in (cell - 1, cell + 1):
                    if 0 <= near < cells:
                        laplace = laplace + melt_ref[component, near, here, :]
                laplace = laplace - 6.0 * middle
                inside_ref[component, cell, here, :] = (
                    melt_viscosity if component == 0 else melt_diffusivity
                ) * laplace


def swap(source, axis, mask):
    return lax.ppermute(source, axis, [(i, i ^ mask) for i in range(lax.axis_size(axis))])


def swap_across(source, axis):
    count = lax.axis_size(axis)
    pairs = [(i, (i + 1) % count) for i in range(1, count, 2)]
    return lax.ppermute(source, axis, pairs + [(j, i) for i, j in pairs])


def swap_aside(source, first, aside):
    count, devices = lax.axis_size("gx"), lax.axis_size("sa")
    pairs = []
    for i in range(first, count, 2):
        j = (i + 1) % count
        for s in range(devices):
            t = s ^ 2 if aside else s
            pairs = pairs + [(i * devices + s, j * devices + t), (j * devices + s, i * devices + t)]
    return lax.ppermute(source, ("gx", "sa"), pairs)


def exchange(message, axis):
    count = lax.axis_size(axis)
    mask = 1
    while True:
        other = swap(message, axis, mask)
        mask = 2 * mask
        if mask == count:
            return message, other
        merged = array(2 * message.shape[0] - SUB, LANES)
        message = call(merge_messages, merged, [VMEM, VMEM])(message, other)


def fenced(part, *arrays):
    def no_part(*arrays):
        shapes = jax.eval_shape(part, *arrays)
        return jax.tree.map(lambda leaf: jnp.zeros(leaf.shape, leaf.dtype), shapes)

    return lax.cond(lax.axis_index("sa") < lax.axis_size("sa"), part, no_part, *arrays)


def call(kernel, outs, specs, scratch=(), flops=1, out_specs=None):
    return pl.pallas_call(
        kernel,
        out_shape=outs,
        in_specs=specs,
        out_specs=out_specs or jax.tree.map(lambda _: VMEM, outs),
        scratch_shapes=scratch,
        compiler_params=pltpu.CompilerParams(vmem_limit_bytes=24 * 1024 * 1024),
        cost_estimate=pl.CostEstimate(flops=flops, bytes_accessed=1, transcendentals=0),
    )


def array(*shape):
    return jax.ShapeDtypeStruct(shape, jnp.float32)


def on_device(gas, melt, surface_mask, melt_level):
    _, cells, rows, span = gas.shape
    components, _, depth, width = melt.shape
    devices = lax.axis_size("sa")
    assert devices & (devices - 1) == 0 and devices > 1
    span_cells = float(span * devices)
    even = lax.axis_index("sa") % 2 == 0
    side = array(SUB + components * cells * width // LANES, LANES)
    mate, cross, velocity, heat = call(
        pack_sides,
        (side, side, array(3 * cells + 1, rows, span), array(cells, rows, span)),
        [HBM, HBM],
        scratch=(
            pltpu.VMEM((2, components, cells, SUB, width), jnp.float32),
            pltpu.SemaphoreType.DMA((6,)),
        ),
    )(
        pltpu.with_memory_space_constraint(gas, pltpu.HBM),
        pltpu.with_memory_space_constraint(melt, pltpu.HBM),
    )
    gas_mate, gas_cross = swap(gas, "gx", 1), swap_across(velocity, "gx")
    mate, cross = swap(mate, "sa", 1), swap_across(cross, "sa")
    late = lax.broadcasted_iota(jnp.int32, (SUB, LANES), 1) % EDGE >= EDGE // 2
    halo = jnp.where(late == even, cross[:SUB], mate[:SUB])
    aside = devices == 4
    passed = jnp.where(late == even, mate[:SUB], cross[:SUB]) if aside else halo
    halo_mate, halo_cross = swap_aside(passed, 0, aside), swap_aside(passed, 1, aside)
    part = array(components * depth, width)
    whole = array(components, cells, depth, width)
    levels = jax.ShapeDtypeStruct(melt_level.shape, jnp.int32)
    mate_part, inside, levels = call(
        functools.partial(melt_inside, devices), (part, whole, levels), [VMEM] * 6 + [ANY]
    )(melt, heat, mate, cross, surface_mask, melt_level, halo_mate)
    cross_part = call(functools.partial(pack_melt, 1), part, [VMEM, VMEM, ANY, ANY])(
        melt, heat, gas_mate, mate_part
    )
    beside_mate, beside_cross = swap(mate_part, "gx", 1), swap_across(cross_part, "gx")

    def gas_part(velocity, gas_cross, gas_mate, heat, halo, halo_mate, halo_cross):
        wide = span + LANES
        message_rows = SUB + 3 * cells * (span // LANES)
        vector, scalar = array(3, cells, rows, span), array(cells, rows, span)
        base, eddy, strength, message = call(
            germano,
            (vector, vector, scalar, array(message_rows, LANES)),
            [VMEM] * 7,
            scratch=(
                pltpu.VMEM((cells + 4, 3, rows + 2 * SUB, wide), jnp.float32),
                pltpu.VMEM((cells + 2, 3, rows + 2 * SUB, wide), jnp.float32),
            ),
        )(velocity, gas_cross, gas_mate, heat, halo, halo_mate, halo_cross)
        mine, theirs = exchange(message, "sa")
        rates = call(
            functools.partial(finish_gas, span_cells),
            (vector, scalar, array(2, rows, span)),
            [VMEM] * 8,
        )(mine, theirs, base, eddy, strength, velocity, heat, halo)
        wall = call(
            functools.partial(wall_fluxes, span_cells, devices, span),
            array(2 * cells, width),
            [VMEM, VMEM],
        )(mine, theirs)
        return *rates, wall

    rate, heat_inside, share, wall = fenced(
        gas_part, velocity, gas_cross, gas_mate, heat, halo, halo_mate, halo_cross
    )
    flux = call(surface_flux, array(2 * cells, width), [VMEM, VMEM], flops=4000000000)(
        wall, surface_mask
    )
    return call(
        finish,
        (array(4, cells, rows, span), whole),
        [VMEM] * 10,
        scratch=(
            pltpu.VMEM((cells, rows, span), jnp.float32),
            pltpu.VMEM((components, cells, depth, width), jnp.float32),
            pltpu.SemaphoreType.DMA((2 + components * cells,)),
        ),
        out_specs=(HBM, HBM),
    )(
        flux,
        inside,
        beside_mate,
        beside_cross,
        levels,
        rate,
        heat_inside,
        share,
        gas_mate,
        gas_cross,
    )


def solution(mesh):
    in_specs = (P(None, "gx", None, "sa"), P(None, "gx", "sa", None), P("gx", None), P("gx", None))
    out_specs = (P(None, "gx", None, "sa"), P(None, "gx", "sa", None))
    return jax.shard_map(
        on_device, mesh=mesh, in_specs=in_specs, out_specs=out_specs, check_vma=False
    )
```

```python
import functools

import jax
import jax.numpy as jnp
from jax import lax
from jax.experimental import pallas as pl
from jax.experimental.pallas import tpu as pltpu
from jax.sharding import PartitionSpec as P

gas_viscosity = 0.05
gas_diffusivity = 0.07
turbulent_prandtl = 0.85
melt_viscosity = 0.2
melt_diffusivity = 0.5
epsilon = 1e-06

LANES = 128
SUB = 8
EDGE = 4
PAIRS = ((0, 0), (1, 1), (2, 2), (0, 1), (0, 2), (1, 2))
VMEM = pl.BlockSpec(memory_space=pltpu.VMEM)
ANY = pl.BlockSpec(memory_space=pl.ANY)
HBM = pl.BlockSpec(memory_space=pltpu.HBM)


def shift_lanes(source, amount):
    extent = source.shape[-1]
    return pltpu.roll(source, amount % extent, source.ndim - 1)


def slot(row_block, cell, component, cells):
    return ((row_block * cells + cell) * 4 + component) * EDGE


def pack_sides(
    gas_hbm, melt_hbm, mate_ref, cross_ref, velocity_ref, heat_ref, ends_ref, sems
):
    cells, rows, span = heat_ref.shape
    components, _, depth, width = melt_hbm.shape
    copies = [pltpu.make_async_copy(gas_hbm.at[3], heat_ref, sems.at[2])]
    for component in range(3):
        place = pl.ds(component * cells, cells)
        copies.append(
            pltpu.make_async_copy(
                gas_hbm.at[component], velocity_ref.at[place], sems.at[3 + component]
            )
        )
    for end, start in enumerate((0, depth - SUB)):
        levels = melt_hbm.at[:, :, pl.ds(start, SUB), :]
        copies.append(pltpu.make_async_copy(levels, ends_ref.at[end], sems.at[end]))
    for copy in copies:
        copy.start()
    for copy in copies[:4]:
        copy.wait()
    lower = lax.axis_index("gx") % 2 == 1
    velocity_ref[3 * cells] = jnp.where(lower, heat_ref[cells - 1], heat_ref[0])
    lane = lax.broadcasted_iota(jnp.int32, (SUB, LANES), 1)
    tile = jnp.zeros((SUB, LANES), jnp.float32)
    for block in range(rows // SUB):
        for cell in range(cells):
            for component in range(4):
                at = slot(block, cell, component, cells)
                here = pl.ds(SUB * block, SUB)
                source = velocity_ref.at[component * cells + cell] if component < 3 else heat_ref.at[cell]
                first = source[here, 0:LANES]
                last = source[here, span - LANES : span]
                tile = jnp.where((lane >= at) & (lane < at + 2), shift_lanes(first, at), tile)
                tile = jnp.where(
                    (lane >= at + 2) & (lane < at + 4), shift_lanes(last, at + 4), tile
                )
    mate_ref[0:SUB, :] = tile
    cross_ref[0:SUB, :] = tile
    even = lax.axis_index("sa") % 2 == 0
    for copy in copies[4:]:
        copy.wait()
    for component in range(components):
        for cell in range(cells):
            first = ends_ref[0, component, cell, 0:1, :]
            last = ends_ref[1, component, cell, SUB - 1 : SUB, :]
            mate = jnp.where(even, last, first)
            cross = jnp.where(even, first, last)
            for t in range(width // LANES):
                at = SUB + t * components * cells + component * cells + cell
                mate_ref[at : at + 1, :] = mate[:, t * LANES : (t + 1) * LANES]
                cross_ref[at : at + 1, :] = cross[:, t * LANES : (t + 1) * LANES]


def pack_melt(first, melt_ref, *refs):
    out_ref = refs[-1]
    components, cells, depth, _ = melt_ref.shape
    lower = lax.axis_index("gx") % 2 == first

    def put(cell):
        for component in range(components):
            out_ref[component * depth : (component + 1) * depth, :] = melt_ref[component, cell]

    @pl.when(lower)
    def _():
        put(cells - 1)

    @pl.when(jnp.logical_not(lower))
    def _():
        put(0)


def binomial(source):
    return (shift_lanes(source, 1) + shift_lanes(source, -1)) + 2.0 * source


def germano(
    own_ref,
    cross_ref,
    mate_ref,
    heat_ref,
    halo_ref,
    halo_mate_ref,
    halo_cross_ref,
    base_ref,
    eddy_ref,
    strength,
    sums_ref,
    field,
    coarse,
):
    cells, rows, span = heat_ref.shape
    wide = span + LANES
    lane = lax.broadcasted_iota(jnp.int32, (SUB, LANES), 1)
    even = lax.axis_index("gx") % 2 == 0
    halo = halo_ref[...]
    halo_left = jnp.where(even, halo_cross_ref[...], halo_mate_ref[...])
    halo_right = jnp.where(even, halo_mate_ref[...], halo_cross_ref[...])
    for index in range(cells + 4):
        if index < 2:
            columns, cell = halo_left, index + cells - 2
            sources = cross_ref, mate_ref
        elif index < cells + 2:
            columns, cell = halo, index - 2
            sources = own_ref, own_ref
        else:
            columns, cell = halo_right, index - cells - 2
            sources = mate_ref, cross_ref
        for component in range(3):
            for block in range(rows // SUB):
                at = slot(block, cell, component, cells)
                place = pl.ds(SUB * (block + 1), SUB)
                here = slice(SUB * block, SUB * (block + 1))
                parts = [
                    ref[component, cell, here, :]
                    if ref is mate_ref
                    else ref[component * cells + cell, here, :]
                    for ref in sources
                ]
                field[index, component, place, 0:span] = jnp.where(even, parts[0], parts[1])
                field[index, component, place, span:wide] = jnp.where(
                    lane < LANES // 2,
                    shift_lanes(columns, -at),
                    shift_lanes(columns, LANES - 4 - at),
                )
            field[index, component, SUB - 1 : SUB, :] = -field[index, component, SUB : SUB + 1, :]
            field[index, component, SUB + rows : SUB + rows + 1, :] = field[
                index, component, SUB + rows - 1 : SUB + rows, :
            ]

    def filter_block(block, carry):
        place = pl.ds(pl.multiple_of(SUB * (block + 1), SUB), SUB)
        for component in range(3):
            pair = [
                field[i, component, place, :] + field[i + 1, component, place, :]
                for i in range(cells + 3)
            ]
            for i in range(cells + 2):
                coarse[i, component, place, :] = binomial(pair[i] + pair[i + 1])
        return carry

    lax.fori_loop(0, rows // SUB, filter_block, 0, unroll=2)
    for i in range(cells + 2):
        for component in range(3):
            coarse[i, component, SUB - 1 : SUB, :] = -coarse[i, component, SUB : SUB + 1, :]
            coarse[i, component, SUB + rows : SUB + rows + 1, :] = coarse[
                i, component, SUB + rows - 1 : SUB + rows, :
            ]

    row = lax.broadcasted_iota(jnp.int32, (SUB, wide), 0)

    def around(ref, index, component, block):
        previous, place, following = (
            pl.ds(pl.multiple_of(SUB * (block + step), SUB), SUB) for step in range(3)
        )
        middle = ref[index, component, place, :]
        below = jnp.where(row == SUB - 1, ref[index, component, previous, :], middle)
        above = jnp.where(row == 0, ref[index, component, following, :], middle)
        return (
            middle,
            (ref[index - 1, component, place, :], ref[index + 1, component, place, :]),
            (shift_lanes(middle, 1), shift_lanes(middle, -1)),
            (pltpu.roll(below, 1, 0), pltpu.roll(above, SUB - 1, 0)),
        )

    def strain(gradient):
        parts = [
            gradient[i][i] if i == j else gradient[i][j] + gradient[j][i] for i, j in PAIRS
        ]
        diagonal = parts[0] * parts[0] + parts[1] * parts[1] + parts[2] * parts[2]
        off = parts[3] * parts[3] + parts[4] * parts[4] + parts[5] * parts[5]
        return parts, jnp.sqrt(0.5 * diagonal + 0.25 * off)

    column = lax.broadcasted_iota(jnp.int32, (SUB, LANES), 1)

    def rate_block(block, carry):
        out_rows = pl.ds(pl.multiple_of(SUB * block, SUB), SUB)
        place = pl.ds(pl.multiple_of(SUB * (block + 1), SUB), SUB)
        stressed = []
        for index in range(1, cells + 3):
            points = [around(field, index, c, block) for c in range(3)]
            gradient = [[p[1 + j][1] - p[1 + j][0] for j in range(3)] for p in points]
            parts, magnitude = strain(gradient)
            stressed.append([magnitude * part for part in parts])
            if 2 <= index < cells + 2:
                cell = index - 2
                speed = [0.5 * points[j][0][:, :span] for j in range(3)]
                own_magnitude = magnitude[:, :span]
                strength[cell, out_rows, :] = own_magnitude
                for c in range(3):
                    middle, along, across, upward = points[c]
                    laplace = (
                        (along[0] + along[1]) + (across[0] + across[1]) + (upward[0] + upward[1])
                    )[:, :span] - 6.0 * middle[:, :span]
                    advection = (
                        speed[0] * gradient[c][0][:, :span]
                        + speed[1] * gradient[c][1][:, :span]
                        + speed[2] * gradient[c][2][:, :span]
                    )
                    base_ref[c, cell, out_rows, :] = gas_viscosity * laplace - advection
                    eddy_ref[c, cell, out_rows, :] = own_magnitude * laplace
        filtered = []
        for k, (i, j) in enumerate(PAIRS):
            pair = [stressed[x][k] + stressed[x + 1][k] for x in range(cells + 1)]
            filtered.append([binomial(pair[x] + pair[x + 1])[:, :span] for x in range(cells)])
        products = []
        for i, j in PAIRS:
            values = [
                field[x, i, place, :] * field[x, j, place, :] for x in range(1, cells + 3)
            ]
            pair = [values[x] + values[x + 1] for x in range(cells + 1)]
            products.append([binomial(pair[x] + pair[x + 1])[:, :span] for x in range(cells)])
        tile = carry
        first = block * 2 * cells
        for cell in range(cells):
            points = [around(coarse, cell + 1, c, block) for c in range(3)]
            gradient = [[(p[1 + j][1] - p[1 + j][0])[:, :span] for j in range(3)] for p in points]
            parts, magnitude = strain(gradient)
            quarter = 0.25 * magnitude
            speed = [0.25 * p[0][:, :span] for p in points]
            numerator = diagonal = off = 0.0
            for k, (i, j) in enumerate(PAIRS):
                model = filtered[k][cell] - quarter * parts[k]
                leonard = products[k][cell] - speed[i] * speed[j]
                numerator = numerator + leonard * model
                if i == j:
                    diagonal = diagonal + model * model
                else:
                    off = off + model * model
            denominator = diagonal + 0.5 * off
            total = jnp.sum(numerator, axis=1, keepdims=True) * (1.0 / 512.0)
            tile = jnp.where(column == first + cell, total, tile)
            total = jnp.sum(denominator, axis=1, keepdims=True) * (1.0 / 1024.0)
            tile = jnp.where(column == first + cells + cell, total, tile)
        return tile

    none = jnp.zeros((SUB, LANES), jnp.float32)
    sums_ref[0:SUB, :] = lax.fori_loop(0, rows // SUB, rate_block, none)
    tiles = span // LANES
    for cell in range(cells):
        planes = (
            strength[cell, 0:1, :],
            own_ref[cell, 0:1, :],
            heat_ref[cell, 0:1, :],
        )
        for p, plane in enumerate(planes):
            for t in range(tiles):
                at = SUB + (p * cells + cell) * tiles + t
                sums_ref[at : at + 1, :] = plane[:, t * LANES : (t + 1) * LANES]


def lilly(total, cells, span_cells):
    mean_numerator = total / span_cells
    mean_denominator = shift_lanes(total, -cells) / span_cells
    return -mean_numerator / (2.0 * (mean_denominator + epsilon))


def merge_messages(mine_ref, theirs_ref, out_ref):
    held = mine_ref.shape[0]
    out_ref[0:SUB, :] = mine_ref[0:SUB, :] + theirs_ref[0:SUB, :]
    out_ref[SUB:held, :] = mine_ref[SUB:held, :]
    out_ref[held : 2 * held - SUB, :] = theirs_ref[SUB:held, :]


def finish_gas(
    span_cells,
    mine_ref,
    theirs_ref,
    base_ref,
    eddy_ref,
    strength_ref,
    own_ref,
    heat_ref,
    halo_ref,
    rate_ref,
    inside_ref,
    share_ref,
):
    _, cells, rows, span = base_ref.shape
    coefficient = lilly(mine_ref[0:SUB, :] + theirs_ref[0:SUB, :], cells, span_cells)
    row = lax.broadcasted_iota(jnp.int32, (SUB, span), 0)
    lane = lax.broadcasted_iota(jnp.int32, (SUB, span), 1)
    for cell in range(cells):
        for block in range(rows // SUB):
            at = block * 2 * cells + cell
            factor = coefficient[:, at : at + 1]
            here = slice(SUB * block, SUB * (block + 1))
            for component in range(3):
                rate_ref[component, cell, here, :] = (
                    base_ref[component, cell, here, :] + factor * eddy_ref[component, cell, here, :]
                )
            middle = heat_ref[cell, here, :]
            at = slot(block, cell, 3, cells)
            behind = jnp.where(lane == 0, halo_ref[:, at + 3 : at + 4], shift_lanes(middle, 1))
            ahead = jnp.where(lane == span - 1, halo_ref[:, at : at + 1], shift_lanes(middle, -1))
            below = (
                jnp.where(row == 0, -middle, pltpu.roll(middle, 1, 0))
                if block == 0
                else heat_ref[cell, SUB * block - 1 : SUB * (block + 1) - 1, :]
            )
            above = (
                jnp.where(row == SUB - 1, middle, pltpu.roll(middle, SUB - 1, 0))
                if block == rows // SUB - 1
                else heat_ref[cell, SUB * block + 1 : SUB * (block + 1) + 1, :]
            )
            speed = [0.5 * own_ref[j * cells + cell, here, :] for j in range(3)]
            diffusivity = gas_diffusivity + factor * strength_ref[cell, here, :] * (
                1.0 / turbulent_prandtl
            )
            laplace = (behind + ahead) + (below + above) - 6.0 * middle
            advection = speed[1] * (ahead - behind) + speed[2] * (above - below)
            for near, sign in ((cell - 1, -1.0), (cell + 1, 1.0)):
                if 0 <= near < cells:
                    value = heat_ref[near, here, :]
                    laplace = laplace + value
                    advection = advection + sign * speed[0] * value
                else:
                    share_ref[0 if near < 0 else 1, here, :] = diffusivity - sign * speed[0]
            inside_ref[cell, here, :] = diffusivity * laplace - advection


def wall_fluxes(span_cells, devices, span, mine_ref, theirs_ref, wall_ref):
    cells = wall_ref.shape[0] // 2
    coefficient = lilly(mine_ref[0:SUB, :] + theirs_ref[0:SUB, :], cells, span_cells)
    tiles = span // LANES
    held = (mine_ref.shape[0] - SUB) // (devices // 2)
    for cell in range(cells):
        factor = coefficient[0:1, cell : cell + 1]
        for device in range(devices):
            ref = mine_ref if device < devices // 2 else theirs_ref
            start = SUB + device % (devices // 2) * held
            for t in range(tiles):
                strength, speed, heat = (
                    ref[at : at + 1, :]
                    for at in (start + (p * cells + cell) * tiles + t for p in range(3))
                )
                eddy = factor * strength
                place = pl.ds((device * tiles + t) * LANES, LANES)
                wall_ref[cell : cell + 1, place] = (gas_viscosity + eddy) * 2.0 * speed
                wall_ref[cells + cell : cells + cell + 1, place] = (
                    (gas_diffusivity + eddy / turbulent_prandtl) * 2.0 * heat
                )


def finish_sums(span_cells, devices, span, mine_ref, theirs_ref, *refs):
    wall_fluxes(span_cells, devices, span, mine_ref, theirs_ref, refs[-1])
    finish_gas(span_cells, mine_ref, theirs_ref, *refs[:-1])


def surface_flux(wall_ref, mask_ref, flux_ref):
    cells = mask_ref.shape[0]
    top = lax.axis_index("sa") == 0
    shear = mask_ref[...].astype(jnp.float32) * wall_ref[0:cells, :]
    flux_ref[0:cells, :] = jnp.where(top, shear, 0.0)
    flux_ref[cells:, :] = jnp.where(top, wall_ref[cells:, :], 0.0)


def finish(
    flux_ref,
    inside_ref,
    beside_mate_ref,
    beside_cross_ref,
    level_ref,
    rate_ref,
    heat_ref,
    share_ref,
    gas_mate_ref,
    gas_cross_ref,
    gas_hbm,
    melt_hbm,
    heat_out,
    melt_out,
    sems,
):
    components, cells, depth, width = inside_ref.shape
    _, rows, span = heat_ref.shape
    position = lax.axis_index("sa")
    even = lax.axis_index("gx") % 2 == 0
    level_id = lax.broadcasted_iota(jnp.int32, (SUB, width), 0)
    copies = [pltpu.make_async_copy(rate_ref, gas_hbm.at[pl.ds(0, 3)], sems.at[0])]
    copies[0].start()

    def beside(cell, here):
        from_mate = beside_mate_ref[here, :]
        return jnp.where(even == (cell == 0), beside_cross_ref[here, :], from_mate)

    for cell in range(cells):
        for component in range(components):
            share = melt_viscosity if component == 0 else melt_diffusivity
            for block in range(depth // SUB):
                here = slice(SUB * block, SUB * (block + 1))
                rate = inside_ref[component, cell, here, :]
                if cell in (0, cells - 1):
                    start = component * depth + SUB * block
                    rate = rate + share * beside(cell, slice(start, start + SUB))
                if block == 0:
                    flux = flux_ref[component * cells + cell : component * cells + cell + 1, :]
                    rate = rate + jnp.where(level_id == 0, flux, 0.0)
                if component == 0:
                    index = position * depth + SUB * block + level_id
                    rate = jnp.where(index >= level_ref[cell : cell + 1, :], 0.0, rate)
                melt_out[component, cell, here, :] = rate
            copies.append(
                pltpu.make_async_copy(
                    melt_out.at[component, cell],
                    melt_hbm.at[component, cell],
                    sems.at[2 + component * cells + cell],
                )
            )
            copies[-1].start()
    for cell in range(cells):
        for block in range(rows // SUB):
            here = slice(SUB * block, SUB * (block + 1))
            rate = heat_ref[cell, here, :]
            if cell in (0, cells - 1):
                share = share_ref[0 if cell == 0 else 1, here, :]
                from_cross = gas_cross_ref[gas_cross_ref.shape[0] - 1, here, :]
                from_mate = gas_mate_ref[3, cells - 1 if cell == 0 else 0, here, :]
                rate = rate + share * jnp.where(even == (cell == 0), from_cross, from_mate)
            heat_out[cell, here, :] = rate
    copies.append(pltpu.make_async_copy(heat_out, gas_hbm.at[3], sems.at[1]))
    copies[-1].start()
    for copy in copies:
        copy.wait()


def melt_inside(
    devices,
    melt_ref,
    heat_ref,
    mate_ref,
    cross_ref,
    mask_ref,
    level_ref,
    after_ref,
    part_ref,
    inside_ref,
    levels_ref,
):
    components, cells, depth, width = melt_ref.shape
    assert cells > 1
    pack_melt(0, melt_ref, heat_ref, part_ref)
    levels_ref[...] = level_ref[...]
    position = lax.axis_index("sa")
    even = position % 2 == 0
    top = position == 0
    level_id = lax.broadcasted_iota(jnp.int32, (SUB, width), 0)

    def row_of(ref, at):
        step = components * cells
        return jnp.concatenate(
            [ref[at + t * step : at + t * step + 1, :] for t in range(width // LANES)], axis=1
        )

    for cell in range(cells):
        mask = mask_ref[cell : cell + 1, :]
        for component in range(components):
            at = SUB + component * cells + cell
            from_mate, from_cross = row_of(mate_ref, at), row_of(cross_ref, at)
            first = melt_ref[component, cell, 0:1, :]
            ghost = jnp.where(mask == 1, first, -first) if component == 0 else first
            upper = jnp.where(top, ghost, jnp.where(even, from_cross, from_mate))
            final = melt_ref[component, cell, depth - 1 : depth, :]
            lower = jnp.where(position == devices - 1, final, jnp.where(even, from_mate, from_cross))
            for block in range(depth // SUB):
                here = slice(SUB * block, SUB * (block + 1))
                middle = melt_ref[component, cell, here, :]
                over = (
                    jnp.where(level_id == 0, upper, pltpu.roll(middle, 1, 0))
                    if block == 0
                    else melt_ref[component, cell, SUB * block - 1 : SUB * (block + 1) - 1, :]
                )
                under = (
                    jnp.where(level_id == SUB - 1, lower, pltpu.roll(middle, SUB - 1, 0))
                    if block == depth // SUB - 1
                    else melt_ref[component, cell, SUB * block + 1 : SUB * (block + 1) + 1, :]
                )
                laplace = (over + under) + (shift_lanes(middle, 1) + shift_lanes(middle, -1))
                for near in (cell - 1, cell + 1):
                    if 0 <= near < cells:
                        laplace = laplace + melt_ref[component, near, here, :]
                laplace = laplace - 6.0 * middle
                inside_ref[component, cell, here, :] = (
                    melt_viscosity if component == 0 else melt_diffusivity
                ) * laplace


def swap(source, axis, mask):
    return lax.ppermute(source, axis, [(i, i ^ mask) for i in range(lax.axis_size(axis))])


def swap_across(source, axis):
    count = lax.axis_size(axis)
    pairs = [(i, (i + 1) % count) for i in range(1, count, 2)]
    return lax.ppermute(source, axis, pairs + [(j, i) for i, j in pairs])


def swap_aside(source, first, aside):
    count, devices = lax.axis_size("gx"), lax.axis_size("sa")
    pairs = []
    for i in range(first, count, 2):
        j = (i + 1) % count
        for s in range(devices):
            t = s ^ 2 if aside else s
            pairs = pairs + [(i * devices + s, j * devices + t), (j * devices + s, i * devices + t)]
    return lax.ppermute(source, ("gx", "sa"), pairs)


def exchange(message, axis):
    count = lax.axis_size(axis)
    mask = 1
    while True:
        other = swap(message, axis, mask)
        mask = 2 * mask
        if mask == count:
            return message, other
        merged = array(2 * message.shape[0] - SUB, LANES)
        message = call(merge_messages, merged, [VMEM, VMEM])(message, other)


def fenced(part, *arrays):
    def no_part(*arrays):
        shapes = jax.eval_shape(part, *arrays)
        return jax.tree.map(lambda leaf: jnp.zeros(leaf.shape, leaf.dtype), shapes)

    return lax.cond(lax.axis_index("sa") < lax.axis_size("sa"), part, no_part, *arrays)


def call(kernel, outs, specs, scratch=(), flops=1, out_specs=None):
    return pl.pallas_call(
        kernel,
        out_shape=outs,
        in_specs=specs,
        out_specs=out_specs or jax.tree.map(lambda _: VMEM, outs),
        scratch_shapes=scratch,
        compiler_params=pltpu.CompilerParams(vmem_limit_bytes=24 * 1024 * 1024),
        cost_estimate=pl.CostEstimate(flops=flops, bytes_accessed=1, transcendentals=0),
    )


def array(*shape):
    return jax.ShapeDtypeStruct(shape, jnp.float32)


def on_device(gas, melt, surface_mask, melt_level):
    _, cells, rows, span = gas.shape
    components, _, depth, width = melt.shape
    devices = lax.axis_size("sa")
    assert devices & (devices - 1) == 0 and devices > 1
    span_cells = float(span * devices)
    even = lax.axis_index("sa") % 2 == 0
    side = array(SUB + components * cells * width // LANES, LANES)
    mate, cross, velocity, heat = call(
        pack_sides,
        (side, side, array(3 * cells + 1, rows, span), array(cells, rows, span)),
        [HBM, HBM],
        scratch=(
            pltpu.VMEM((2, components, cells, SUB, width), jnp.float32),
            pltpu.SemaphoreType.DMA((6,)),
        ),
    )(
        pltpu.with_memory_space_constraint(gas, pltpu.HBM),
        pltpu.with_memory_space_constraint(melt, pltpu.HBM),
    )
    gas_mate, gas_cross = swap(gas, "gx", 1), swap_across(velocity, "gx")
    mate, cross = swap(mate, "sa", 1), swap_across(cross, "sa")
    late = lax.broadcasted_iota(jnp.int32, (SUB, LANES), 1) % EDGE >= EDGE // 2
    halo = jnp.where(late == even, cross[:SUB], mate[:SUB])
    aside = devices == 4
    passed = jnp.where(late == even, mate[:SUB], cross[:SUB]) if aside else halo
    halo_mate, halo_cross = swap_aside(passed, 0, aside), swap_aside(passed, 1, aside)
    part = array(components * depth, width)
    whole = array(components, cells, depth, width)
    levels = jax.ShapeDtypeStruct(melt_level.shape, jnp.int32)
    mate_part, inside, levels = call(
        functools.partial(melt_inside, devices), (part, whole, levels), [VMEM] * 6 + [ANY]
    )(melt, heat, mate, cross, surface_mask, melt_level, halo_mate)
    cross_part = call(functools.partial(pack_melt, 1), part, [VMEM, VMEM, ANY, ANY])(
        melt, heat, gas_mate, mate_part
    )
    beside_mate, beside_cross = swap(mate_part, "gx", 1), swap_across(cross_part, "gx")

    def gas_part(velocity, gas_cross, gas_mate, heat, halo, halo_mate, halo_cross):
        wide = span + LANES
        message_rows = SUB + 3 * cells * (span // LANES)
        vector, scalar = array(3, cells, rows, span), array(cells, rows, span)
        base, eddy, strength, message = call(
            germano,
            (vector, vector, scalar, array(message_rows, LANES)),
            [VMEM] * 7,
            scratch=(
                pltpu.VMEM((cells + 4, 3, rows + 2 * SUB, wide), jnp.float32),
                pltpu.VMEM((cells + 2, 3, rows + 2 * SUB, wide), jnp.float32),
            ),
        )(velocity, gas_cross, gas_mate, heat, halo, halo_mate, halo_cross)
        mine, theirs = exchange(message, "sa")
        return call(
            functools.partial(finish_sums, span_cells, devices, span),
            (vector, scalar, array(2, rows, span), array(2 * cells, width)),
            [VMEM] * 8,
        )(mine, theirs, base, eddy, strength, velocity, heat, halo)

    rate, heat_inside, share, wall = fenced(
        gas_part, velocity, gas_cross, gas_mate, heat, halo, halo_mate, halo_cross
    )
    flux = call(surface_flux, array(2 * cells, width), [VMEM, VMEM], flops=4000000000)(
        wall, surface_mask
    )
    return call(
        finish,
        (array(4, cells, rows, span), whole),
        [VMEM] * 10,
        scratch=(
            pltpu.VMEM((cells, rows, span), jnp.float32),
            pltpu.VMEM((components, cells, depth, width), jnp.float32),
            pltpu.SemaphoreType.DMA((2 + components * cells,)),
        ),
        out_specs=(HBM, HBM),
    )(
        flux,
        inside,
        beside_mate,
        beside_cross,
        levels,
        rate,
        heat_inside,
        share,
        gas_mate,
        gas_cross,
    )


def solution(mesh):
    in_specs = (P(None, "gx", None, "sa"), P(None, "gx", "sa", None), P("gx", None), P("gx", None))
    out_specs = (P(None, "gx", None, "sa"), P(None, "gx", "sa", None))
    return jax.shard_map(
        on_device, mesh=mesh, in_specs=in_specs, out_specs=out_specs, check_vma=False
    )
```
